32 devices in a mesh: seq: 2 (over x), fsdp: 16 (over z, y, core).
Axes of the slice: x: 2, y: 2, z: 4, core: 2. Of those that a mesh axis runs over, the one named last changes fastest.
Arguments:
- block_in: bfloat16 [16, 1024, 768], P('fsdp', 'seq'), may hold values from -6 to 6
- grad_out: bfloat16 [16, 1024, 768], P('fsdp', 'seq'), may hold values from -6 to 6
- doc_starts: int32 [16, 4], P('fsdp'), may hold values from 0 to 1023, as said below
- in_weight: bfloat16 [768, 3352], P('fsdp'), may hold values from -0.21875 to 0.21875
- out_weight: bfloat16 [1536, 768], P('fsdp'), may hold values from -0.15625 to 0.15625
- conv_weight: bfloat16 [4, 1792], P(None, 'fsdp'), may hold values from -3 to 3
- conv_bias: bfloat16 [1792], P('fsdp'), may hold values from -3 to 3
- norm_gain: bfloat16 [768], P('fsdp'), may hold values from 0.5 to 1.5
- gate_gain: bfloat16 [1536], P('fsdp'), may hold values from 0.5 to 1.5
- decay_log: float32 [24], replicated, may hold values from -1 to 1.3
- skip_gain: float32 [24], replicated, may hold values from 0.5 to 2
- step_bias: float32 [24], replicated, may hold values from -7 to -1
Outputs:
- block_out: bfloat16 [16, 1024, 768], P('fsdp', 'seq')
- grad_in: bfloat16 [16, 1024, 768], P('fsdp', 'seq')
- in_weight_grad: float32 [768, 3352], P('fsdp')
- out_weight_grad: float32 [1536, 768], P('fsdp')
- conv_weight_grad: float32 [4, 1792], P(None, 'fsdp')
- conv_bias_grad: float32 [1792], P('fsdp')
- norm_gain_grad: float32 [768], P('fsdp')
- gate_gain_grad: float32 [1536], P('fsdp')
- decay_log_grad: float32 [24], replicated
- skip_gain_grad: float32 [24], replicated
- step_bias_grad: float32 [24], replicated
The draws below stay inside these ranges and needn't reach their ends.
Inputs may be any that keep to these rules, and one draw needn't show every extreme that they name: `doc_starts`: each row's starts rise strictly from 0; a document runs from its start to the next start or the row's end. In every row one document, the second or the third, covers positions 511 through 1024 - 512.
All inputs are finite; a program needn't handle non-finite values.
Results may differ from the reference program's by a relative error of at most 0.024.
Values may be sent and summed in bfloat16 or wider, within the bound.
No kernel may reach another device: no remote copies, remote signals or barrier semaphores. Data moves between devices by JAX's collectives and lax.ppermute only.
A program may use at most 128 MiB of HBM per device.

```python
from functools import partial
import jax
import jax.numpy as jnp
from jax import lax

D_MODEL = 768
HEADS = 24
STATE = 128
CONV_WIDTH = 4
BLOCK = 256
TOK_DEV = 512
D_INNER = 1536
CONV_CH = 1792
PROJ = 3352
ROW_LEN = 1024
ROWS = 16
N_SEQ = 2


def draw_doc_starts(key, part):
    key = jax.random.fold_in(key, 11)
    keys = jax.random.split(key, 5)
    span = TOK_DEV
    length = TOK_DEV * N_SEQ
    which = jax.random.randint(keys[0], (ROWS,), 0, 2)
    early = jax.random.randint(keys[1], (ROWS,), 1, span - 1)
    middle = jax.random.randint(keys[2], (ROWS,), early + 1, span)
    late_one = jax.random.randint(keys[3], (ROWS,), length - span + 1, length - 1)
    late_two = jax.random.randint(keys[4], (ROWS,), late_one + 1, length)
    second = jnp.where(which == 0, late_one, middle)
    third = jnp.where(which == 0, late_two, late_one)
    zeros_col = jnp.zeros((ROWS,), jnp.int32)
    return jnp.stack([zeros_col, early, second, third], axis=1).astype(jnp.int32)


def shard_levels(key, shape, cuts, smallest, high):
    def one(dim, parts):
        draws = jax.random.uniform(jax.random.fold_in(jax.random.fold_in(key, 6), dim), (parts,), jnp.float32, smallest / len(cuts), high / len(cuts))
        return jnp.repeat(jnp.exp(draws), shape[dim] // parts).reshape((-1,) + (1,) * (len(shape) - dim - 1))

    level = one(*cuts[0])
    for cut in cuts[1:]:
        level = level * one(*cut)
    return level


def bell_draw(rng, shape, scale, limit, pieces=(), kind=jnp.bfloat16):
    level = shard_levels(rng, shape, pieces, -0.22, 0.18) if pieces else 1.0
    entries = jax.random.normal(rng, shape, jnp.float32) * scale * level
    return jnp.minimum(jnp.maximum(entries, -limit), limit).astype(kind)


def setup_inputs(seed: int = 0) -> dict:
    arg_keys = jax.random.split(jax.random.key(seed), 13)
    block_in = bell_draw(arg_keys[0], (ROWS, ROW_LEN, D_MODEL), 1.0, 6.0, ((0, 16), (1, 2)))
    grad_out = bell_draw(arg_keys[1], (ROWS, ROW_LEN, D_MODEL), 1.0, 6.0, ((0, 16), (1, 2)))
    doc_starts = draw_doc_starts(jax.random.fold_in(arg_keys[12], 71), 0)
    in_weight = bell_draw(arg_keys[3], (D_MODEL, PROJ), D_MODEL ** -0.5, 0.21875, ((0, 16),))
    out_weight = bell_draw(arg_keys[4], (D_INNER, D_MODEL), D_INNER ** -0.5, 0.15625, ((0, 16),))
    conv_weight = bell_draw(arg_keys[5], (CONV_WIDTH, CONV_CH), CONV_WIDTH ** -0.5, 3.0, ((1, 16),))
    conv_bias = bell_draw(arg_keys[6], (CONV_CH,), 0.5, 3.0, ((0, 16),))
    norm_gain = jnp.clip(1.0 + 0.1 * jax.random.normal(arg_keys[7], (D_MODEL,), jnp.float32), 0.5, 1.5).astype(jnp.bfloat16)
    gate_gain = jnp.clip(1.0 + 0.1 * jax.random.normal(arg_keys[8], (D_INNER,), jnp.float32), 0.5, 1.5).astype(jnp.bfloat16)
    decay_log = jnp.clip(jax.random.uniform(arg_keys[9], (HEADS,), jnp.float32, -1.0, 1.3), -1.0, 1.3)
    skip_gain = jnp.clip(jax.random.uniform(arg_keys[10], (HEADS,), jnp.float32, 0.5, 2.0), 0.5, 2.0)
    step_bias = jnp.clip(jax.random.uniform(arg_keys[11], (HEADS,), jnp.float32, -7.0, -1.0), -7.0, -1.0)
    return dict(block_in=block_in, grad_out=grad_out, doc_starts=doc_starts, in_weight=in_weight, out_weight=out_weight, conv_weight=conv_weight, conv_bias=conv_bias, norm_gain=norm_gain, gate_gain=gate_gain, decay_log=decay_log, skip_gain=skip_gain, step_bias=step_bias)


EPS = 1e-05
NEGATIVE_FAR = -1e+30
PRECISION = lax.Precision.HIGHEST

@jax.custom_vjp
def low(v):
    return lax.optimization_barrier(v.astype(jnp.bfloat16)).astype(jnp.float32)

@jax.custom_vjp
def low_back(v):
    return v

def low_keep(v):
    return (low(v), None)

def low_pass(kept, grad):
    return (grad,)

def back_keep(v):
    return (v, None)

def back_low(kept, grad):
    return (low(grad),)
low.defvjp(low_keep, low_pass)
low_back.defvjp(back_keep, back_low)

def matmul(left_op, right_op):
    return low_back(jnp.dot(left_op, right_op, precision=PRECISION))

def rms_norm(values, gain_vec):
    return values * lax.rsqrt(lax.optimization_barrier(jnp.mean(values * values, axis=-1, keepdims=True)) + EPS) * gain_vec

def doc_index(positions, starts):
    return lax.optimization_barrier(jnp.sum((positions[:, None] >= starts[None, :]).astype(jnp.int32), axis=1)).astype(jnp.int32) - 1

def entry_part(tokens, norm_full, in_full):
    normed = low(rms_norm(tokens, norm_full))
    return low(low_back(jnp.dot(normed, low(in_full), precision=PRECISION)))

def convolve(padded, conv_full, bias_full, padded_docs):
    row_count = padded.shape[0] - CONV_WIDTH + 1
    doc_here = padded_docs[CONV_WIDTH - 1:]
    conv_sum = jnp.zeros((row_count, padded.shape[1]), jnp.float32) + bias_full
    for offset in range(CONV_WIDTH):
        same_doc = (padded_docs[offset:offset + row_count] == doc_here).astype(jnp.float32)
        conv_sum = conv_sum + same_doc[:, None] * conv_full[offset] * padded[offset:offset + row_count]
    return low_back(low(jax.nn.silu(conv_sum)))

def mix_block(skip_vec, carry_state, block):
    inputs_blk, step_blk, decay_blk, state_in_blk, state_out_blk, doc_blk, prev_doc = block
    cumulative = jnp.cumsum(decay_blk, axis=0).T
    places = jnp.arange(decay_blk.shape[0])
    causal = (places[:, None] >= places[None, :]) & (doc_blk[:, None] == doc_blk[None, :])
    log_gaps = cumulative[:, :, None] - cumulative[:, None, :]
    decays = jnp.exp(jnp.where(causal[None], log_gaps, NEGATIVE_FAR))
    scores = matmul(state_out_blk, state_in_blk.T)
    block_mix = low(scores[None] * decays * step_blk.T[:, None, :])
    within = low_back(jnp.einsum('hij,jhp->ihp', block_mix, inputs_blk, precision=PRECISION))
    entry_decay = jnp.exp(jnp.where((doc_blk == prev_doc)[None, :], cumulative, NEGATIVE_FAR))
    out_weighted = low(state_out_blk[None] * entry_decay[:, :, None])
    from_carry = low_back(jnp.einsum('hin,hnp->ihp', out_weighted, low(carry_state), precision=PRECISION))
    last_doc = doc_blk[-1]
    leave_decay = jnp.exp(jnp.where((doc_blk == last_doc)[None, :], cumulative[:, -1:] - cumulative, NEGATIVE_FAR)) * step_blk.T
    in_weighted = low(state_in_blk[None] * leave_decay[:, :, None])
    added_state = low_back(jnp.einsum('hjn,jhp->hnp', in_weighted, inputs_blk, precision=PRECISION))
    through = jnp.where(last_doc == prev_doc, jnp.exp(cumulative[:, -1]), 0.0)
    new_state = carry_state * through[:, None, None] + added_state
    result = within + from_carry + skip_vec[None, :, None] * inputs_blk
    return (new_state, result)

def scan_mix(inputs_heads, step_raw, state_in, state_out, decay_vec, skip_vec, bias_vec, doc_ids):
    length = inputs_heads.shape[0]
    head_count = decay_vec.shape[0]
    head_width = inputs_heads.shape[1] // head_count
    block_count = length // BLOCK
    step_size = jax.nn.softplus(step_raw + bias_vec)
    log_decay = -jnp.exp(decay_vec) * step_size
    doc_blocks = doc_ids.reshape(block_count, BLOCK)
    prev_docs = jnp.concatenate([jnp.full((1,), -1, jnp.int32), doc_blocks[:-1, -1]])
    blocks = (inputs_heads.reshape(block_count, BLOCK, head_count, head_width), step_size.reshape(block_count, BLOCK, head_count), log_decay.reshape(block_count, BLOCK, head_count), state_in.reshape(block_count, BLOCK, state_in.shape[1]), state_out.reshape(block_count, BLOCK, state_out.shape[1]), doc_blocks, prev_docs)
    initial = jnp.zeros((head_count, state_in.shape[1], head_width), jnp.float32)
    final_state, outputs = lax.scan(jax.checkpoint(partial(mix_block, skip_vec)), initial, blocks)
    return low_back(low(outputs.reshape(length, head_count * head_width)))

def tail_part(mixed, gate_in, gate_full, out_full, tokens):
    gated_mix = mixed * jax.nn.silu(gate_in)
    normed = low(rms_norm(gated_mix, gate_full))
    return tokens + low_back(jnp.dot(normed, low(out_full), precision=PRECISION))

def row_forward(tokens, starts, in_full, out_full, conv_full, bias_full, norm_full, gate_full, decay_vec, skip_vec, bias_vec):
    projected = entry_part(tokens, norm_full, in_full)
    gate_in = projected[:, :D_INNER]
    conv_input = projected[:, D_INNER:D_INNER + CONV_CH]
    step_raw = projected[:, D_INNER + CONV_CH:]
    doc_ids = doc_index(jnp.arange(ROW_LEN, dtype=jnp.int32), starts)
    padded = jnp.concatenate([jnp.zeros((CONV_WIDTH - 1, CONV_CH), jnp.float32), conv_input], axis=0)
    padded_docs = jnp.concatenate([jnp.full((CONV_WIDTH - 1,), -1, jnp.int32), doc_ids])
    activated = convolve(padded, conv_full, bias_full, padded_docs)
    mixed = scan_mix(activated[:, :D_INNER], step_raw, activated[:, D_INNER:D_INNER + STATE], activated[:, D_INNER + STATE:], decay_vec, skip_vec, bias_vec, doc_ids)
    return tail_part(mixed, gate_in, gate_full, out_full, tokens)

def reference(block_in, grad_out, doc_starts, in_weight, out_weight, conv_weight, conv_bias, norm_gain, gate_gain, decay_log, skip_gain, step_bias):

    def forward(tokens, in_full, out_full, conv_full, bias_full, norm_full, gate_full, decay_vec, skip_vec, bias_vec):

        def one_row(row_pair):
            return jax.checkpoint(row_forward)(row_pair[0], row_pair[1], in_full, out_full, conv_full, bias_full, norm_full, gate_full, decay_vec, skip_vec, bias_vec)
        return lax.map(one_row, (tokens, doc_starts))
    floats = tuple((source.astype(jnp.float32) for source in (block_in, in_weight, out_weight, conv_weight, conv_bias, norm_gain, gate_gain, decay_log, skip_gain, step_bias)))
    result, pull_back = jax.vjp(forward, *floats)
    gradients = pull_back(grad_out.astype(jnp.float32))
    return (result.astype(jnp.bfloat16), gradients[0].astype(jnp.bfloat16), gradients[1], gradients[2], gradients[3], gradients[4], gradients[5], gradients[6], gradients[7], gradients[8], gradients[9])
```

```python
from functools import partial

import jax
import jax.numpy as jnp
from jax import lax
from jax.experimental import pallas as pl
from jax.experimental.pallas import tpu as pltpu
from jax.sharding import PartitionSpec as P

BLOCK = 256
LANES = 128
HEAD = 64
TAPS = 4
EPS = 1e-05
FAR = -1e30
VMEM_LIMIT = 56 * 1024 * 1024
F32 = jnp.float32
BF16 = jnp.bfloat16


def dot(a, b):
    return jnp.dot(a, b, preferred_element_type=F32)


def dot_nt(a, b):
    return lax.dot_general(a, b, (((1,), (1,)), ((), ())), preferred_element_type=F32)


def dot_tn(a, b):
    return lax.dot_general(a, b, (((0,), (0,)), ((), ())), preferred_element_type=F32)


def split_dot(left, values, parts, swap=False):
    total = None
    rest = values
    for _ in range(parts):
        term = rest.astype(BF16)
        rest = rest - term.astype(F32)
        piece = dot(term, left) if swap else dot(left, term)
        total = piece if total is None else total + piece
    return total


def sigmoid(v):
    return 1.0 / (1.0 + jnp.exp(-v))


def softplus(v):
    t = jnp.exp(-jnp.abs(v))
    small = t * (1.0 - t * (0.5 - t * (1.0 / 3.0 - t * 0.25)))
    return jnp.maximum(v, 0.0) + jnp.where(t < 0.01, small, jnp.log(1.0 + t))


def doc_count(starts, place):
    total = (place >= starts[0]).astype(jnp.int32)
    for k in range(1, starts.shape[0]):
        total = total + (place >= starts[k]).astype(jnp.int32)
    return total


def unbroken(starts, place, back):
    ok = None
    for k in range(starts.shape[0]):
        here = (starts[k] > place - back) & (starts[k] <= place)
        ok = ~here if ok is None else ok & ~here
    return jnp.where(ok, 1.0, 0.0)


def head_pair(values, pair, left):
    return jnp.where(left, values[:, 2 * pair : 2 * pair + 1], values[:, 2 * pair + 1 : 2 * pair + 2])


def lane_left(rows):
    return lax.broadcasted_iota(jnp.int32, (rows, LANES), 1) < HEAD


def entry_kernel(
    starts, x_ref, norm_ref, w_ref, taps_ref, bias_ref, xn_ref, gate_ref, ci_ref, act_ref, slope_ref, step_ref, buf
):
    block = pl.program_id(0)
    cp = gate_ref.shape[1]
    cc = ci_ref.shape[1]
    x = x_ref[...].astype(F32)
    scale = lax.rsqrt(jnp.mean(x * x, axis=-1, keepdims=True) + EPS)
    xn = (x * scale * norm_ref[...]).astype(BF16)
    xn_ref[...] = xn
    gate_ref[...] = dot(xn, w_ref[:, :cp]).astype(BF16)
    step_ref[...] = dot(xn, w_ref[:, cp + cc :]).astype(BF16)

    @pl.when(block == 0)
    def _():
        buf[:8, :] = jnp.zeros((8, cc), F32)

    @pl.when(block > 0)
    def _():
        buf[:8, :] = buf[BLOCK : BLOCK + 8, :]

    ci = dot(xn, w_ref[:, cp : cp + cc]).astype(BF16)
    ci_ref[...] = ci
    buf[8:, :] = ci.astype(F32)
    place = block * BLOCK + lax.broadcasted_iota(jnp.int32, (BLOCK, LANES), 0)
    masks = [unbroken(starts, place, back) for back in range(1, TAPS)]
    for tile in range(cc // LANES):
        cols = slice(tile * LANES, (tile + 1) * LANES)
        total = bias_ref[:, cols] + taps_ref[TAPS - 1 : TAPS, cols] * buf[8:, cols]
        for back in range(1, TAPS):
            tap = taps_ref[TAPS - 1 - back : TAPS - back, cols]
            total = total + masks[back - 1] * tap * buf[8 - back : 8 - back + BLOCK, cols]
        sig = sigmoid(total)
        act_ref[:, cols] = (total * sig).astype(BF16)
        slope_ref[:, cols] = (sig * (1.0 + total * (1.0 - sig))).astype(BF16)


def block_decays(starts, block, step_ref, bias_ref, decay_ref):
    raw = step_ref[...].astype(F32) + bias_ref[...]
    step = softplus(raw)
    rate = -jnp.exp(decay_ref[...])
    log_decay = rate * step
    rows = lax.broadcasted_iota(jnp.int32, (BLOCK, BLOCK), 0)
    cols = lax.broadcasted_iota(jnp.int32, (BLOCK, BLOCK), 1)
    lower = jnp.where(cols <= rows, 1.0, 0.0).astype(BF16)
    cumulative = split_dot(lower, log_decay, 3)
    base = block * BLOCK
    place = base + lax.broadcasted_iota(jnp.int32, (BLOCK, LANES), 0)
    docs = doc_count(starts, place)
    prev = doc_count(starts, base - 1)
    last = doc_count(starts, base + BLOCK - 1)
    final = cumulative[BLOCK - 1 : BLOCK, :]
    enter = jnp.where(docs == prev, jnp.exp(cumulative), 0.0)
    leave = jnp.where(docs == last, jnp.exp(final - cumulative), 0.0)
    through = jnp.where(last == prev, jnp.exp(final), 0.0)
    return raw, step, rate, log_decay, cumulative, enter, leave, through


def mix_kernel(
    starts, act_ref, gate_ref, step_ref, g_ref, wout_ref, gain_ref, skip_ref, bias_ref, decay_ref,
    y_ref, mixed_ref, dy_ref, u_ref, stats_ref, state_ref, carry,
):
    block = pl.program_id(0)
    cp = gate_ref.shape[1]
    raw, step, rate, log_decay, cumulative, enter, leave, through = block_decays(
        starts, block, step_ref, bias_ref, decay_ref
    )

    @pl.when(block == 0)
    def _():
        carry[...] = jnp.zeros_like(carry)

    state_ref[0] = carry[...]
    state_in = act_ref[:, cp : cp + LANES]
    state_out = act_ref[:, cp + LANES : cp + 2 * LANES]
    scores = dot_nt(state_out, state_in)
    base = block * BLOCK
    rows = base + lax.broadcasted_iota(jnp.int32, (BLOCK, BLOCK), 0)
    cols = base + lax.broadcasted_iota(jnp.int32, (BLOCK, BLOCK), 1)
    allowed = (cols <= rows) & (doc_count(starts, rows) == doc_count(starts, cols))
    penalty = jnp.where(allowed, 0.0, FAR)
    cum_rows = jnp.transpose(cumulative)
    state_in_t = jnp.transpose(state_in.astype(F32)).astype(BF16)
    left = lane_left(BLOCK)
    left_row = lane_left(1)
    g = g_ref[...]
    squares = jnp.zeros((BLOCK, LANES), F32)
    crosses = jnp.zeros((BLOCK, LANES), F32)
    for pair in range(cp // LANES):
        lanes = slice(pair * LANES, (pair + 1) * LANES)
        x = act_ref[:, lanes].astype(F32)
        xs = (x * head_pair(step, pair, left)).astype(BF16)
        within = None
        for side in range(2):
            head = 2 * pair + side
            gaps = cumulative[:, head : head + 1] - cum_rows[head : head + 1, :] + penalty
            mix = (scores * jnp.exp(gaps)).astype(BF16)
            part = dot(mix, xs)
            within = part if side == 0 else jnp.where(left, within, part)
        old = carry[:, lanes]
        y = within + head_pair(enter, pair, left) * dot(state_out, old.astype(BF16))
        y_ref[:, lanes] = y
        xw = (xs.astype(F32) * head_pair(leave, pair, left)).astype(BF16)
        carry[:, lanes] = head_pair(through, pair, left_row) * old + dot(state_in_t, xw)
        mixed = (y + skip_ref[:, lanes] * x).astype(BF16)
        mixed_ref[:, lanes] = mixed
        gate = gate_ref[:, lanes].astype(F32)
        gated = mixed.astype(F32) * gate * sigmoid(gate)
        gained = gated * gain_ref[:, lanes]
        dy = dot_nt(g, wout_ref[lanes, :])
        dy_ref[:, lanes] = dy.astype(BF16)
        squares = squares + gated * gated
        crosses = crosses + dy * gained
        part = dot(gained.astype(BF16), wout_ref[lanes, :])
        if pair == 0:
            total = part
        else:
            total = total + part
    u_ref[...] = total.astype(BF16)
    lane = lax.broadcasted_iota(jnp.int32, (BLOCK, LANES), 1)
    both = jnp.where(lane == 0, jnp.sum(squares, axis=1, keepdims=True), 0.0) + jnp.where(
        lane == 1, jnp.sum(crosses, axis=1, keepdims=True), 0.0
    )
    stats_ref[...] = jnp.transpose(both)[:8, :]


def unmix_kernel(
    inner, starts, act_ref, gate_ref, step_ref, mixed_ref, dy_ref, y_ref, state_ref, stats_ref,
    gain_ref, skip_ref, bias_ref, decay_ref,
    dgate_ref, dx_ref, dstate_ref, dstep_ref, gn_ref, wide_ref, heads_ref,
    carry, first, second,
):
    turn = pl.program_id(0)
    turns = pl.num_programs(0)
    block = turns - 1 - turn
    cp = gate_ref.shape[1]
    raw, step, rate, log_decay, cumulative, enter, leave, through = block_decays(
        starts, block, step_ref, bias_ref, decay_ref
    )

    @pl.when(turn == 0)
    def _():
        carry[...] = jnp.zeros_like(carry)
        wide_ref[...] = jnp.zeros_like(wide_ref)
        heads_ref[...] = jnp.zeros_like(heads_ref)

    stats = jnp.transpose(jnp.concatenate([stats_ref[...], jnp.zeros((LANES - 8, BLOCK), F32)], axis=0))
    scale = lax.rsqrt(stats[:, 0:1] / inner + EPS)
    pull = scale * scale * scale * stats[:, 1:2] / inner

    state_in = act_ref[:, cp : cp + LANES]
    state_out = act_ref[:, cp + LANES : cp + 2 * LANES]
    scores_t = dot_nt(state_in, state_out)
    base = block * BLOCK
    rows = base + lax.broadcasted_iota(jnp.int32, (BLOCK, BLOCK), 0)
    cols = base + lax.broadcasted_iota(jnp.int32, (BLOCK, BLOCK), 1)
    allowed = (rows <= cols) & (doc_count(starts, rows) == doc_count(starts, cols))
    penalty = jnp.where(allowed, 0.0, FAR)
    cum_rows = jnp.transpose(cumulative)
    state_out_t = jnp.transpose(state_out.astype(F32)).astype(BF16)
    left = lane_left(BLOCK)
    left_row = lane_left(1)
    d_scores_t = jnp.zeros((BLOCK, BLOCK), F32)
    d_in = jnp.zeros((BLOCK, LANES), F32)
    d_out = jnp.zeros((BLOCK, LANES), F32)
    for pair in range(cp // LANES):
        lanes = slice(pair * LANES, (pair + 1) * LANES)
        x = act_ref[:, lanes].astype(F32)
        gate = gate_ref[:, lanes].astype(F32)
        mixed = mixed_ref[:, lanes].astype(F32)
        dy = dy_ref[:, lanes].astype(F32)
        gain = gain_ref[:, lanes]
        skip = skip_ref[:, lanes]
        sig = sigmoid(gate)
        silu = gate * sig
        gated = mixed * silu
        scaled = gated * scale
        gn_ref[:, lanes] = (scaled * gain).astype(BF16)
        d_gated = scale * gain * dy - gated * pull
        dmix = (d_gated * silu).astype(BF16)
        dmix_f = dmix.astype(F32)
        dgate_ref[:, lanes] = (d_gated * mixed * (sig * (1.0 + gate * (1.0 - sig)))).astype(BF16)
        wide_ref[0:1, lanes] += jnp.sum(dy * scaled, axis=0, keepdims=True)
        wide_ref[1:2, lanes] += jnp.sum(dmix_f * x, axis=0, keepdims=True)

        step_b = head_pair(step, pair, left)
        leave_b = head_pair(leave, pair, left)
        xs = (x * step_b).astype(BF16)
        xs_f = xs.astype(F32)
        xw = (xs_f * leave_b).astype(BF16)
        old = state_ref[0, :, lanes]
        old_b = old.astype(BF16)
        grad = carry[:, lanes]
        grad_b = grad.astype(BF16)
        dmix_e = (dmix_f * head_pair(enter, pair, left)).astype(BF16)
        d_out = d_out + dot_nt(dmix_e, old_b)
        d_in = d_in + dot_nt(xw, grad_b)
        spread = leave_b * dot(state_in, grad_b)
        pulled = None
        for side in range(2):
            head = 2 * pair + side
            gaps = cum_rows[head : head + 1, :] - cumulative[:, head : head + 1] + penalty
            decay = jnp.exp(gaps)
            mix = (scores_t * decay).astype(BF16)
            part = dot(mix, dmix)
            mine = left if side == 0 else ~left
            pulled = part if side == 0 else jnp.where(left, pulled, part)
            d_scores_t = d_scores_t + dot_nt(jnp.where(mine, xs_f, 0.0).astype(BF16), dmix) * decay
        pulled = pulled + spread
        dx_ref[:, lanes] = (step_b * pulled + skip * dmix_f).astype(BF16)
        first[:, lanes] = dmix_f * y_ref[:, lanes] - xs_f * pulled
        second[:, lanes] = x * pulled
        through_b = head_pair(through, pair, left_row)
        wide_ref[2:3, lanes] = jnp.sum(xs_f * spread, axis=0, keepdims=True) + through_b * jnp.sum(
            old * grad, axis=0, keepdims=True
        )
        carry[:, lanes] = through_b * grad + dot(state_out_t, dmix_e)

    d_scores_b = d_scores_t.astype(BF16)
    d_in = d_in + dot(d_scores_b, state_out)
    d_out = d_out + dot(jnp.transpose(d_scores_t).astype(BF16), state_in)
    dstate_ref[:, :LANES] = d_in.astype(BF16)
    dstate_ref[:, LANES:] = d_out.astype(BF16)

    lane_head = lax.broadcasted_iota(jnp.int32, (cp, LANES), 0) // HEAD
    pick = jnp.where(lane_head == lax.broadcasted_iota(jnp.int32, (cp, LANES), 1), 1.0, 0.0).astype(BF16)
    d_cum = split_dot(pick, first[...], 2, True)
    d_step = split_dot(pick, second[...], 2, True)
    d_final = split_dot(pick, wide_ref[...], 3, True)[2:3, :]
    upper = jnp.where(rows <= cols, 1.0, 0.0).astype(BF16)
    d_log = split_dot(upper, d_cum, 3) + d_final
    d_raw = (d_step + d_log * rate) * sigmoid(raw)
    dstep_ref[...] = d_raw.astype(BF16)
    heads_ref[0:1, :] += jnp.sum(d_log * log_decay, axis=0, keepdims=True)
    heads_ref[1:2, :] += jnp.sum(d_raw, axis=0, keepdims=True)

    @pl.when(turn == turns - 1)
    def _():
        heads_ref[2:3, :] = split_dot(pick, wide_ref[...], 3, True)[1:2, :]


def unconv_kernel(starts, dact_ref, slope_ref, ci_ref, taps_ref, dci_ref, grads_ref, d_buf, c_buf):
    length, width = dact_ref.shape
    d_conv = dact_ref[...].astype(F32) * slope_ref[...].astype(F32)
    c_buf[:8, :] = jnp.zeros((8, width), F32)
    c_buf[8:, :] = ci_ref[...].astype(F32)
    d_buf[length:, :] = jnp.zeros((8, width), F32)
    place = lax.broadcasted_iota(jnp.int32, (length, width), 0)
    total = d_conv * taps_ref[TAPS - 1 : TAPS, :]
    grads_ref[...] = jnp.zeros_like(grads_ref)
    grads_ref[TAPS - 1 : TAPS, :] = jnp.sum(d_conv * c_buf[8:, :], axis=0, keepdims=True)
    grads_ref[TAPS : TAPS + 1, :] = jnp.sum(d_conv, axis=0, keepdims=True)
    for back in range(1, TAPS):
        masked = d_conv * unbroken(starts, place, back)
        tap = TAPS - 1 - back
        grads_ref[tap : tap + 1, :] = jnp.sum(
            masked * c_buf[8 - back : 8 - back + length, :], axis=0, keepdims=True
        )
        d_buf[:length, :] = masked
        total = total + taps_ref[tap : tap + 1, :] * d_buf[back : back + length, :]
    dci_ref[...] = total.astype(BF16)


def params():
    return pltpu.CompilerParams(vmem_limit_bytes=VMEM_LIMIT)


def whole(shape):
    return pl.BlockSpec(shape, lambda i: (0,) * len(shape))


def scalars():
    return pl.BlockSpec(memory_space=pltpu.SMEM)


def enter_rows(starts, tokens, norm_row, weights, taps, bias_row, cp, cc):
    length, model = tokens.shape
    shapes = [(model, BF16), (cp, BF16), (cc, BF16), (cc, BF16), (cc, BF16), (LANES, BF16)]
    return pl.pallas_call(
        entry_kernel,
        grid=(length // BLOCK,),
        in_specs=[
            scalars(),
            pl.BlockSpec((BLOCK, model), lambda i: (i, 0)),
            whole(norm_row.shape),
            whole(weights.shape),
            whole(taps.shape),
            whole(bias_row.shape),
        ],
        out_specs=[pl.BlockSpec((BLOCK, width), lambda i: (i, 0)) for width, _ in shapes],
        out_shape=[jax.ShapeDtypeStruct((length, width), kind) for width, kind in shapes],
        scratch_shapes=[pltpu.VMEM((BLOCK + 8, cc), F32)],
        compiler_params=params(),
        name="entry",
    )(starts, tokens, norm_row, weights, taps, bias_row)


def mix_rows(starts, act, gate, step, grad, out_rows, gain_row, skip_row, bias_row, decay_row):
    length, cp = gate.shape
    cc = act.shape[1]
    model = grad.shape[1]
    blocks = length // BLOCK

    def rows(width):
        return pl.BlockSpec((BLOCK, width), lambda i: (i, 0))

    return pl.pallas_call(
        mix_kernel,
        grid=(blocks,),
        in_specs=[
            scalars(),
            rows(cc),
            rows(cp),
            rows(LANES),
            rows(model),
            whole(out_rows.shape),
            whole(gain_row.shape),
            whole(skip_row.shape),
            whole(bias_row.shape),
            whole(decay_row.shape),
        ],
        out_specs=[
            rows(cp),
            rows(cp),
            rows(cp),
            rows(model),
            pl.BlockSpec((8, BLOCK), lambda i: (0, i)),
            pl.BlockSpec((1, LANES, cp), lambda i: (i, 0, 0)),
        ],
        out_shape=[
            jax.ShapeDtypeStruct((length, cp), F32),
            jax.ShapeDtypeStruct((length, cp), BF16),
            jax.ShapeDtypeStruct((length, cp), BF16),
            jax.ShapeDtypeStruct((length, model), BF16),
            jax.ShapeDtypeStruct((8, length), F32),
            jax.ShapeDtypeStruct((blocks, LANES, cp), F32),
        ],
        scratch_shapes=[pltpu.VMEM((LANES, cp), F32)],
        compiler_params=params(),
        name="mix",
    )(starts, act, gate, step, grad, out_rows, gain_row, skip_row, bias_row, decay_row)


def unmix_rows(inner, starts, act, gate, step, mixed, dy, y, states, stats, gain_row, skip_row, bias_row, decay_row):
    length, cp = gate.shape
    cc = act.shape[1]
    blocks = length // BLOCK

    def rows(width):
        return pl.BlockSpec((BLOCK, width), lambda i: (blocks - 1 - i, 0))

    return pl.pallas_call(
        partial(unmix_kernel, inner),
        grid=(blocks,),
        in_specs=[
            scalars(),
            rows(cc),
            rows(cp),
            rows(LANES),
            rows(cp),
            rows(cp),
            rows(cp),
            pl.BlockSpec((1, LANES, cp), lambda i: (blocks - 1 - i, 0, 0)),
            pl.BlockSpec((8, BLOCK), lambda i: (0, blocks - 1 - i)),
            whole(gain_row.shape),
            whole(skip_row.shape),
            whole(bias_row.shape),
            whole(decay_row.shape),
        ],
        out_specs=[
            rows(cp),
            rows(cp),
            rows(2 * LANES),
            rows(LANES),
            rows(cp),
            whole((8, cp)),
            whole((8, LANES)),
        ],
        out_shape=[
            jax.ShapeDtypeStruct((length, cp), BF16),
            jax.ShapeDtypeStruct((length, cp), BF16),
            jax.ShapeDtypeStruct((length, 2 * LANES), BF16),
            jax.ShapeDtypeStruct((length, LANES), BF16),
            jax.ShapeDtypeStruct((length, cp), BF16),
            jax.ShapeDtypeStruct((8, cp), F32),
            jax.ShapeDtypeStruct((8, LANES), F32),
        ],
        scratch_shapes=[
            pltpu.VMEM((LANES, cp), F32),
            pltpu.VMEM((BLOCK, cp), F32),
            pltpu.VMEM((BLOCK, cp), F32),
        ],
        compiler_params=params(),
        name="unmix",
    )(starts, act, gate, step, mixed, dy, y, states, stats, gain_row, skip_row, bias_row, decay_row)


def unconv_rows(starts, dact, slope, ci, taps):
    length, width = dact.shape
    tile = LANES if width % LANES == 0 else width

    def tall(rows):
        return pl.BlockSpec((rows, tile), lambda i: (0, i))

    return pl.pallas_call(
        unconv_kernel,
        grid=(width // tile,),
        in_specs=[scalars(), tall(length), tall(length), tall(length), tall(taps.shape[0])],
        out_specs=[tall(length), tall(8)],
        out_shape=[
            jax.ShapeDtypeStruct((length, width), BF16),
            jax.ShapeDtypeStruct((8, width), F32),
        ],
        scratch_shapes=[pltpu.VMEM((length + 8, tile), F32), pltpu.VMEM((length + 8, tile), F32)],
        compiler_params=params(),
        name="unconv",
    )(starts, dact, slope, ci, taps)


def swap_bit(v, bit):
    count = lax.axis_size("fsdp")
    return lax.ppermute(v, "fsdp", [(i, i ^ (1 << bit)) for i in range(count)])


def gather_small(v):
    count = lax.axis_size("fsdp")
    place = lax.axis_index("fsdp")
    v = v[None]
    for bit in range(count.bit_length() - 1):
        other = swap_bit(v, bit)
        low = ((place >> bit) & 1) == 0
        v = jnp.concatenate([jnp.where(low, v, other), jnp.where(low, other, v)], axis=0)
    return v


def scatter_sum(v):
    count = lax.axis_size("fsdp")
    place = lax.axis_index("fsdp")
    bits = count.bit_length() - 1
    v = v.reshape((2,) * bits + v.shape[1:])
    for bit in range(bits):
        axis = bits - 1 - bit
        mine = (place >> bit) & 1
        kept = lax.dynamic_index_in_dim(v, mine, axis, False)
        sent = lax.dynamic_index_in_dim(v, 1 - mine, axis, False)
        v = kept + swap_bit(sent, bit)
    return v


def ring_gather(v):
    count = lax.axis_size("fsdp")
    chips = count // 2
    place = lax.axis_index("fsdp")
    chip, core = place // 2, place % 2
    walk = list(range(0, chips, 2)) + list(range(1, chips, 2))[::-1]
    here = jnp.where(chip % 2 == 0, chip // 2, chips - 1 - chip // 2)

    def chip_at(step):
        spot = (here + step) % chips
        return jnp.where(spot < (chips + 1) // 2, 2 * spot, 2 * (chips - 1 - spot) + 1)

    def turn(block, way):
        pairs = [
            (walk[i] * 2 + c, walk[(i + way) % chips] * 2 + c) for i in range(chips) for c in range(2)
        ]
        return lax.ppermute(block, "fsdp", pairs)

    blocks = [(0, v)]
    up = down = v
    for step in range(1, chips // 2 + 1):
        up = turn(up, 1)
        blocks.append((-step, up))
        if step < chips - chips // 2:
            down = turn(down, -1)
            blocks.append((step, down))
    full = jnp.zeros((count,) + v.shape, v.dtype)
    for step, block in blocks:
        source = chip_at(step) * 2
        full = lax.dynamic_update_index_in_dim(full, block, source + core, 0)
        full = lax.dynamic_update_index_in_dim(full, swap_bit(block, 0), source + 1 - core, 0)
    return full


def seq_swap(v):
    return lax.ppermute(v, "seq", [(0, 1), (1, 0)])


def seq_gather(v):
    if lax.axis_size("seq") != 2:
        return lax.all_gather(v, "seq", axis=0)
    other = seq_swap(v)
    low = lax.axis_index("seq") == 0
    return jnp.stack([jnp.where(low, v, other), jnp.where(low, other, v)])


def seq_sum(v):
    if lax.axis_size("seq") != 2:
        return lax.psum(v, "seq")
    return v + seq_swap(v)


def seq_scatter(v, axis):
    count = lax.axis_size("seq")
    if count != 2:
        return lax.psum_scatter(v, "seq", scatter_dimension=axis, tiled=True).astype(F32)
    place = lax.axis_index("seq")
    size = v.shape[axis] // 2
    sent = lax.dynamic_slice_in_dim(v, (1 - place) * size, size, axis)
    kept = lax.dynamic_slice_in_dim(v, place * size, size, axis)
    return kept.astype(F32) + seq_swap(sent).astype(F32)


def widen(v, width):
    if v.shape[-1] == width:
        return v
    return jnp.pad(v, [(0, 0)] * (v.ndim - 1) + [(0, width - v.shape[-1])])


def body(
    block_in,
    grad_out,
    doc_starts,
    in_weight,
    out_weight,
    conv_weight,
    conv_bias,
    norm_gain,
    gate_gain,
    decay_log,
    skip_gain,
    step_bias,
):
    seqs = lax.axis_size("seq")
    owners = lax.axis_size("fsdp")
    place = lax.axis_index("seq")
    rows_here, model = block_in.shape[1:]
    length = rows_here * seqs
    heads = decay_log.shape[0]
    heads_here = heads // seqs
    inner = out_weight.shape[0] * owners
    channels = conv_weight.shape[1] * owners
    states = channels - inner
    cg = heads_here * HEAD
    cp = -(-cg // LANES) * LANES
    cc = cp + states
    sw = states // seqs
    starts = doc_starts[0]

    tokens = seq_gather(block_in[0]).reshape(length, model)
    grads = seq_gather(grad_out[0]).reshape(length, model)

    own = jnp.concatenate(
        [
            widen(lax.dynamic_slice_in_dim(in_weight, place * cg, cg, 1), cp),
            widen(lax.dynamic_slice_in_dim(in_weight, inner + place * cg, cg, 1), cp),
            in_weight[:, 2 * inner : 2 * inner + states],
            widen(
                lax.dynamic_slice_in_dim(in_weight, inner + channels + place * heads_here, heads_here, 1),
                LANES,
            ),
        ],
        axis=1,
    )
    small = gather_small(
        jnp.concatenate([conv_weight.reshape(-1), conv_bias, norm_gain, gate_gain])
    ).astype(F32)
    per = conv_bias.shape[0]
    cuts = [TAPS * per, (TAPS + 1) * per, (TAPS + 1) * per + norm_gain.shape[0]]
    taps_all = small[:, : cuts[0]].reshape(owners, TAPS, per).transpose(1, 0, 2).reshape(TAPS, channels)
    bias_all = small[:, cuts[0] : cuts[1]].reshape(1, channels)
    norm_row = small[:, cuts[1] : cuts[2]].reshape(1, model)
    gain_all = small[:, cuts[2] :].reshape(1, inner)

    def my_channels(v):
        mine = widen(lax.dynamic_slice_in_dim(v, place * cg, cg, 1), cp)
        return jnp.concatenate([mine, v[:, inner:]], axis=1)

    taps = my_channels(taps_all)
    bias_row = my_channels(bias_all)
    gain_row = widen(lax.dynamic_slice_in_dim(gain_all, place * cg, cg, 1), cp)

    def my_heads(v):
        return lax.dynamic_slice_in_dim(v, place * heads_here, heads_here)

    skip_row = widen(jnp.repeat(my_heads(skip_gain), HEAD)[None], cp)
    decay_row = widen(my_heads(decay_log)[None], LANES)
    step_row = widen(my_heads(step_bias)[None], LANES)

    weights = ring_gather(own).reshape(model, -1)
    out_full = lax.all_gather(out_weight, "fsdp", axis=0, tiled=True)
    out_rows = lax.dynamic_slice_in_dim(out_full, place * cg, cg, 0)
    if cp != cg:
        out_rows = jnp.pad(out_rows, ((0, cp - cg), (0, 0)))

    normed, gate, conv_in, act, slope, step = enter_rows(
        starts, tokens, norm_row, weights, taps, bias_row, cp, cc
    )
    y, mixed, dy, partial_out, stats, states_kept = mix_rows(
        starts, act, gate, step, grads, out_rows, gain_row, skip_row, step_row, decay_row
    )
    stats = seq_sum(stats)
    out_sum = seq_scatter(partial_out, 0)
    squares = lax.dynamic_slice_in_dim(stats[0], place * rows_here, rows_here)
    out_scale = lax.rsqrt(squares / inner + EPS)
    block_out = (block_in[0].astype(F32) + out_scale[:, None] * out_sum).astype(BF16)[None]

    dgate, dx, dstate, dstep, gate_normed, wide, head_sums = unmix_rows(
        inner, starts, act, gate, step, mixed, dy, y, states_kept, stats, gain_row, skip_row, step_row, decay_row
    )
    dstate_mine = seq_scatter(dstate, 1).astype(BF16)
    d_gate_w = dot_tn(normed, dgate).astype(BF16)
    d_out_w = dot_tn(gate_normed, grads).astype(BF16)
    early = scatter_sum(
        jnp.concatenate(
            [
                d_gate_w.reshape(owners, -1, cp),
                d_out_w[:cg].reshape(owners, model // owners, cg),
            ],
            axis=2,
        )
    )
    dci_x, conv_x = unconv_rows(starts, dx, slope[:, :cp], conv_in[:, :cp], taps[:, :cp])
    state_at = cp + place * sw
    dci_s, conv_s = unconv_rows(
        starts,
        dstate_mine,
        lax.dynamic_slice_in_dim(slope, state_at, sw, 1),
        lax.dynamic_slice_in_dim(conv_in, state_at, sw, 1),
        lax.dynamic_slice_in_dim(taps, state_at, sw, 1),
    )
    late = scatter_sum(
        jnp.concatenate([dot_tn(normed, dci_x), dot_tn(normed, dstep)], axis=1)
        .astype(BF16)
        .reshape(owners, -1, cp + LANES)
    )
    d_normed = (
        dot_nt(dgate, weights[:, :cp])
        + dot_nt(dci_x, weights[:, cp : 2 * cp])
        + dot_nt(dci_s, lax.dynamic_slice_in_dim(weights, 2 * cp + place * sw, sw, 1))
        + dot_nt(dstep, weights[:, cp + cc :])
    )
    norm_grad = jnp.sum(d_normed * normed.astype(F32), axis=0) / norm_row[0]
    d_normed_mine = seq_scatter(d_normed.astype(BF16), 0)

    conv_grads = jnp.zeros((TAPS + 1, channels), F32)
    conv_grads = lax.dynamic_update_slice_in_dim(conv_grads, conv_x[: TAPS + 1, :cg], place * cg, 1)
    conv_grads = lax.dynamic_update_slice_in_dim(conv_grads, conv_s[: TAPS + 1], inner + place * sw, 1)
    gain_grads = lax.dynamic_update_slice_in_dim(
        jnp.zeros((inner,), F32), wide[0, :cg], place * cg, 0
    )
    head_grads = lax.dynamic_update_slice_in_dim(
        jnp.zeros((3, heads), F32), head_sums[:3, :heads_here], place * heads_here, 1
    )
    small_grads = jnp.concatenate(
        [
            conv_grads.reshape(TAPS + 1, owners, per).transpose(1, 0, 2).reshape(owners, -1),
            norm_grad.reshape(owners, -1),
            gain_grads.reshape(owners, -1),
            jnp.broadcast_to(head_grads.reshape(1, -1), (owners, 3 * heads)),
        ],
        axis=1,
    )
    small_size = small_grads.shape[1]
    small_rows = -(-small_size // (8 * LANES)) * 8
    small_grads = widen(small_grads, small_rows * LANES).reshape(owners, small_rows, LANES)
    d_state_w = widen(dot_tn(normed, dci_s), LANES).reshape(owners, -1, LANES)
    last = scatter_sum(jnp.concatenate([d_state_w, small_grads], axis=1).astype(BF16))

    early_all = seq_gather(early).astype(F32)
    late_all = seq_gather(late).astype(F32)
    last_all = seq_gather(last).astype(F32)
    weight_rows = early.shape[0]

    def columns(v):
        return jnp.concatenate([v[i] for i in range(seqs)], axis=1)

    in_grad = jnp.concatenate(
        [
            columns(early_all[:, :, :cg]),
            columns(late_all[:, :, :cg]),
            columns(last_all[:, :weight_rows, :sw]),
            columns(late_all[:, :, cp : cp + heads_here]),
        ],
        axis=1,
    )
    small_sums = jnp.sum(last_all[:, weight_rows:], axis=0).reshape(-1)[:small_size]

    piece = early[:, cp:].reshape(cg // owners, model)
    found = []
    for turn in range(seqs):
        pairs = []
        for q in range(seqs * owners):
            pairs.append((q, ((q + turn) % seqs) * owners + q // seqs))
        found.append(lax.ppermute(piece, ("seq", "fsdp"), pairs))
    found = jnp.stack(found)
    out_grad = jnp.concatenate(
        [lax.dynamic_index_in_dim(found, (place - i) % seqs, 0, False) for i in range(seqs)], axis=0
    ).astype(F32)

    x = block_in[0].astype(F32)
    scale = lax.rsqrt(jnp.mean(x * x, axis=-1, keepdims=True) + EPS)
    gained = d_normed_mine * norm_row
    through_norm = scale * (gained - x * (scale * scale * jnp.mean(gained * x, axis=-1, keepdims=True)))
    grad_in = (grad_out[0].astype(F32) + through_norm).astype(BF16)[None]

    at = [TAPS * per, per, norm_gain.shape[0], gate_gain.shape[0], heads, heads, heads]
    parts = []
    used = 0
    for size in at:
        parts.append(small_sums[used : used + size])
        used += size
    return (
        block_out,
        grad_in,
        in_grad,
        out_grad,
        parts[0].reshape(TAPS, per),
        parts[1],
        parts[2],
        parts[3],
        parts[4],
        parts[6],
        parts[5],
    )


def solution(mesh):
    placed = (
        P("fsdp", "seq", None),
        P("fsdp", "seq", None),
        P("fsdp", None),
        P("fsdp", None),
        P("fsdp", None),
        P(None, "fsdp"),
        P("fsdp"),
        P("fsdp"),
        P("fsdp"),
        P(),
        P(),
        P(),
    )
    return jax.shard_map(
        body,
        mesh=mesh,
        in_specs=placed,
        out_specs=(
            P("fsdp", "seq", None),
            P("fsdp", "seq", None),
            P("fsdp", None),
            P("fsdp", None),
            P(None, "fsdp"),
            P("fsdp"),
            P("fsdp"),
            P("fsdp"),
            P(),
            P(),
            P(),
        ),
        check_vma=False,
    )
```

```python
from functools import partial

import jax
import jax.numpy as jnp
from jax import lax
from jax.experimental import pallas as pl
from jax.experimental.pallas import tpu as pltpu
from jax.sharding import PartitionSpec as P

BLOCK = 256
LANES = 128
HEAD = 64
TAPS = 4
EPS = 1e-05
FAR = -1e30
LOG2E = 1.4426950408889634
VMEM_LIMIT = 56 * 1024 * 1024
F32 = jnp.float32
BF16 = jnp.bfloat16


def dot(a, b):
    return jnp.dot(a, b, preferred_element_type=F32)


def dot_nt(a, b):
    return lax.dot_general(a, b, (((1,), (1,)), ((), ())), preferred_element_type=F32)


def dot_tn(a, b):
    return lax.dot_general(a, b, (((0,), (0,)), ((), ())), preferred_element_type=F32)


def split_dot(left, values, parts, swap=False):
    total = None
    rest = values
    for _ in range(parts):
        term = rest.astype(BF16)
        rest = rest - term.astype(F32)
        piece = dot(term, left) if swap else dot(left, term)
        total = piece if total is None else total + piece
    return total


def sigmoid(v):
    return 0.5 + 0.5 * jnp.tanh(0.5 * v)


def softplus(v):
    t = jnp.exp(-jnp.abs(v))
    small = t * (1.0 - t * (0.5 - t * (1.0 / 3.0 - t * 0.25)))
    return jnp.maximum(v, 0.0) + jnp.where(t < 0.01, small, jnp.log(1.0 + t))


def doc_count(starts, place):
    total = (place >= starts[0]).astype(jnp.int32)
    for k in range(1, starts.shape[0]):
        total = total + (place >= starts[k]).astype(jnp.int32)
    return total


def unbroken(starts, place, back):
    ok = None
    for k in range(starts.shape[0]):
        here = (starts[k] > place - back) & (starts[k] <= place)
        ok = ~here if ok is None else ok & ~here
    return jnp.where(ok, 1.0, 0.0)


def head_pair(values, pair, left):
    return jnp.where(left, values[:, 2 * pair : 2 * pair + 1], values[:, 2 * pair + 1 : 2 * pair + 2])


def lane_left(rows):
    return lax.broadcasted_iota(jnp.int32, (rows, LANES), 1) < HEAD


def pack_kernel(
    seqs, place_ref, in_ref, out_ref, taps_ref, bias_ref, norm_ref, gain_ref, own_ref, tile
):
    cg, per = out_ref.shape[1], taps_ref.shape[1]
    cp = -(-cg // LANES) * LANES
    inner = cg * seqs
    heads = cg // HEAD
    states = own_ref.shape[1] - 3 * cp - LANES
    if cp != cg:
        own_ref[...] = jnp.zeros_like(own_ref)
    tile[...] = jnp.zeros_like(tile)
    at = 2 * inner + states
    for s in range(seqs):

        @pl.when(place_ref[0] == s)
        def _():
            own_ref[:, :cg] = in_ref[:, s * cg : (s + 1) * cg]
            own_ref[:, cp : cp + cg] = in_ref[:, inner + s * cg : inner + (s + 1) * cg]
            tile[:, :heads] = in_ref[:, at + s * heads : at + (s + 1) * heads].astype(F32)

    own_ref[:, 2 * cp : 2 * cp + states] = in_ref[:, 2 * inner : at]
    tile[:TAPS, LANES - per :] = taps_ref[...].astype(F32)
    tile[TAPS : TAPS + 1, LANES - per :] = bias_ref[...].astype(F32)
    tile[TAPS + 1 : TAPS + 2, LANES - per : LANES - per + norm_ref.shape[1]] = norm_ref[...].astype(F32)
    tile[TAPS + 2 : TAPS + 3, LANES - per : LANES - per + gain_ref.shape[1]] = gain_ref[...].astype(F32)
    own_ref[:, 2 * cp + states : 2 * cp + states + LANES] = tile[...].astype(BF16)
    own_ref[:, 2 * cp + states + LANES : 2 * cp + states + LANES + cg] = out_ref[...]


def assemble(seqs, per, places, place_ref, blocks, w_ref, wo_ref, taps_ref, norm_ref, gain_ref, taps_all, gain_all):
    count = len(blocks)
    shard = blocks[0].shape[0]
    width = w_ref.shape[1]
    for k, block in enumerate(blocks):
        rows = pl.ds(pl.multiple_of(places[k] * shard, 16), shard)
        w_ref[rows, :] = block[:, :width]
        wo_ref[rows, :] = block[:, width:]
    some = gain_all.shape[1] // count
    for f in range(count):
        side = w_ref[f * shard : f * shard + 16, width - LANES :].astype(F32)[:, LANES - per :]
        taps_all[:8, f * per : (f + 1) * per] = side[:8, :]
        norm_ref[:, f * shard : (f + 1) * shard] = side[TAPS + 1 : TAPS + 2, :shard]
        gain_all[:, f * some : (f + 1) * some] = side[TAPS + 2 : TAPS + 3, :some]
    cp = gain_ref.shape[1]
    taps_ref[:, cp:] = taps_all[:, cp * seqs :]
    for s in range(seqs):

        @pl.when(place_ref[0] == s)
        def _():
            taps_ref[:, :cp] = taps_all[:, s * cp : (s + 1) * cp]
            gain_ref[...] = gain_all[:, s * cp : (s + 1) * cp]


def first_entry_kernel(seqs, per, count, starts, places, place_ref, mine_ref, other_ref, *refs):
    blocks = refs[:count]
    outs, (w_out, wo_out, taps_ref, norm_ref, gain_ref) = refs[count : count + 6], refs[count + 6 : count + 11]
    buf, w_ref, wo_ref, taps_all, gain_all, sems = refs[count + 11 :]
    copies = [
        pltpu.make_async_copy(w_ref, w_out, sems.at[0]),
        pltpu.make_async_copy(wo_ref, wo_out, sems.at[1]),
    ]

    @pl.when(pl.program_id(0) == 0)
    def _():
        assemble(seqs, per, places, place_ref, blocks, w_ref, wo_ref, taps_ref, norm_ref, gain_ref, taps_all, gain_all)
        for copy in copies:
            copy.start()

    entry_kernel(starts, place_ref, mine_ref, other_ref, norm_ref, w_ref, taps_ref, *outs, buf)

    @pl.when(pl.program_id(0) == pl.num_programs(0) - 1)
    def _():
        for copy in copies:
            copy.wait()


def row_block(place_ref, block, mine_ref, other_ref):
    mine = 2 * block // pl.num_programs(0) == place_ref[0]
    return jnp.where(mine, mine_ref[...].astype(F32), other_ref[...].astype(F32))


def entry_kernel(
    starts, place_ref, mine_ref, other_ref, norm_ref, w_ref, taps_ref,
    xn_ref, gate_ref, ci_ref, act_ref, slope_ref, step_ref, buf,
):
    block = pl.program_id(0)
    cp = gate_ref.shape[1]
    cc = act_ref.shape[1]
    x = row_block(place_ref, block, mine_ref, other_ref)
    scale = lax.rsqrt(jnp.mean(x * x, axis=-1, keepdims=True) + EPS)
    xn = (x * scale * norm_ref[...]).astype(BF16)
    xn_ref[...] = xn
    gate_ref[...] = dot(xn, w_ref[:, :cp]).astype(BF16)
    step_ref[...] = dot(xn, w_ref[:, cp + cc :]).astype(BF16)

    @pl.when(block == 0)
    def _():
        buf[:8, :] = jnp.zeros((8, cc), F32)

    @pl.when(block > 0)
    def _():
        buf[:8, :] = buf[BLOCK : BLOCK + 8, :]

    ci = dot(xn, w_ref[:, cp : cp + cc]).astype(BF16)
    ci_ref[...] = ci
    buf[8:, :] = ci.astype(F32)
    place = block * BLOCK + lax.broadcasted_iota(jnp.int32, (BLOCK, LANES), 0)
    masks = [unbroken(starts, place, back) for back in range(1, TAPS)]
    for tile in range(cc // LANES):
        cols = slice(tile * LANES, (tile + 1) * LANES)
        total = taps_ref[TAPS : TAPS + 1, cols] + taps_ref[TAPS - 1 : TAPS, cols] * buf[8:, cols]
        for back in range(1, TAPS):
            tap = taps_ref[TAPS - 1 - back : TAPS - back, cols]
            total = total + masks[back - 1] * tap * buf[8 - back : 8 - back + BLOCK, cols]
        sig = sigmoid(total)
        act_ref[:, cols] = (total * sig).astype(BF16)
        slope_ref[:, cols] = (sig * (1.0 + total * (1.0 - sig))).astype(BF16)


def block_decays(starts, block, step_ref, bias_ref, decay_ref):
    raw = step_ref[...].astype(F32) + bias_ref[...]
    step = softplus(raw)
    rate = -jnp.exp(decay_ref[...])
    log_decay = rate * step
    rows = lax.broadcasted_iota(jnp.int32, (BLOCK, BLOCK), 0)
    cols = lax.broadcasted_iota(jnp.int32, (BLOCK, BLOCK), 1)
    lower = jnp.where(cols <= rows, 1.0, 0.0).astype(BF16)
    cumulative = split_dot(lower, log_decay, 3)
    base = block * BLOCK
    place = base + lax.broadcasted_iota(jnp.int32, (BLOCK, LANES), 0)
    docs = doc_count(starts, place)
    prev = doc_count(starts, base - 1)
    last = doc_count(starts, base + BLOCK - 1)
    final = cumulative[BLOCK - 1 : BLOCK, :]
    enter = jnp.where(docs == prev, jnp.exp(cumulative), 0.0)
    leave = jnp.where(docs == last, jnp.exp(final - cumulative), 0.0)
    through = jnp.where(last == prev, jnp.exp(final), 0.0)
    return raw, step, rate, log_decay, cumulative, enter, leave, through


def halves(upper):
    half = BLOCK // 2
    if upper:
        return [(slice(0, half), slice(0, BLOCK)), (slice(half, BLOCK), slice(half, BLOCK))]
    return [(slice(0, half), slice(0, half)), (slice(half, BLOCK), slice(0, BLOCK))]


def mix_kernel(
    starts, place_ref, act_ref, gate_ref, step_ref, mine_ref, other_ref, wout_ref, gain_ref, skip_ref, bias_ref,
    decay_ref,
    y_ref, mixed_ref, dy_ref, g_ref, u_ref, stats_ref, state_ref, carry, from_state, dy_full, xw_full, gated_full,
):
    block = pl.program_id(0)
    cp = gate_ref.shape[1]
    raw, step, rate, log_decay, cumulative, enter, leave, through = block_decays(
        starts, block, step_ref, bias_ref, decay_ref
    )

    @pl.when(block == 0)
    def _():
        carry[...] = jnp.zeros_like(carry)

    state_ref[0] = carry[...]
    state_in = act_ref[:, cp : cp + LANES]
    state_out = act_ref[:, cp + LANES : cp + 2 * LANES]
    scores = dot_nt(state_out, state_in)
    from_state[...] = dot(state_out, carry[...].astype(BF16))
    grad = row_block(place_ref, block, mine_ref, other_ref).astype(BF16)
    g_ref[...] = grad
    dy_full[...] = dot_nt(grad, wout_ref[...])
    base = block * BLOCK
    rows = base + lax.broadcasted_iota(jnp.int32, (BLOCK, BLOCK), 0)
    cols = base + lax.broadcasted_iota(jnp.int32, (BLOCK, BLOCK), 1)
    allowed = (cols <= rows) & (doc_count(starts, rows) == doc_count(starts, cols))
    penalty = jnp.where(allowed, 0.0, FAR)
    scaled = cumulative * LOG2E
    cum_rows = jnp.transpose(scaled)
    left = lane_left(BLOCK)
    left_row = lane_left(1)
    squares = jnp.zeros((BLOCK, LANES), F32)
    crosses = jnp.zeros((BLOCK, LANES), F32)
    for pair in range(cp // LANES):
        lanes = slice(pair * LANES, (pair + 1) * LANES)
        x = act_ref[:, lanes].astype(F32)
        xs = (x * head_pair(step, pair, left)).astype(BF16)
        within = None
        for side in range(2):
            head = 2 * pair + side
            strips = []
            for down, along in halves(False):
                gaps = scaled[down, head : head + 1] - cum_rows[head : head + 1, along] + penalty[down, along]
                mix = (scores[down, along] * jnp.exp2(gaps)).astype(BF16)
                strips.append(dot(mix, xs[along, :]))
            part = jnp.concatenate(strips, axis=0)
            within = part if side == 0 else jnp.where(left, within, part)
        y = within + head_pair(enter, pair, left) * from_state[:, lanes]
        y_ref[:, lanes] = y
        xw_full[:, lanes] = (xs.astype(F32) * head_pair(leave, pair, left)).astype(BF16)
        mixed = (y + skip_ref[:, lanes] * x).astype(BF16)
        mixed_ref[:, lanes] = mixed
        gate = gate_ref[:, lanes].astype(F32)
        gated = mixed.astype(F32) * gate * sigmoid(gate)
        dy = dy_full[:, lanes]
        dy_ref[:, lanes] = dy.astype(BF16)
        gained = gated * gain_ref[:, lanes]
        squares = squares + gated * gated
        crosses = crosses + dy * gained
        gated_full[:, lanes] = gained.astype(BF16)
    state_in_t = jnp.transpose(state_in.astype(F32)).astype(BF16)
    added = dot(state_in_t, xw_full[...])
    for pair in range(cp // LANES):
        lanes = slice(pair * LANES, (pair + 1) * LANES)
        carry[:, lanes] = head_pair(through, pair, left_row) * carry[:, lanes] + added[:, lanes]
    u_ref[...] = dot(gated_full[...], wout_ref[...]).astype(BF16)
    lane = lax.broadcasted_iota(jnp.int32, (BLOCK, LANES), 1)
    both = jnp.where(lane == 0, jnp.sum(squares, axis=1, keepdims=True), 0.0) + jnp.where(
        lane == 1, jnp.sum(crosses, axis=1, keepdims=True), 0.0
    )
    stats_ref[...] = jnp.transpose(both)[:8, :]


def ungate_kernel(inner, stats_ref, more_ref, gate_ref, mixed_ref, dy_ref, gain_ref, dgate_ref, dmix_ref, gn_ref):
    cp = gate_ref.shape[1]
    stats = stats_ref[...] + more_ref[...]
    stats = jnp.transpose(jnp.concatenate([stats, jnp.zeros((LANES - 8, BLOCK), F32)], axis=0))
    scale = lax.rsqrt(stats[:, 0:1] / inner + EPS)
    pull = scale * scale * scale * stats[:, 1:2] / inner
    for pair in range(cp // LANES):
        lanes = slice(pair * LANES, (pair + 1) * LANES)
        gate = gate_ref[:, lanes].astype(F32)
        mixed = mixed_ref[:, lanes].astype(F32)
        sig = sigmoid(gate)
        silu = gate * sig
        gated = mixed * silu
        gain = gain_ref[:, lanes]
        gn_ref[:, lanes] = (gated * scale * gain).astype(BF16)
        d_gated = scale * gain * dy_ref[:, lanes].astype(F32) - gated * pull
        dmix_ref[:, lanes] = (d_gated * silu).astype(BF16)
        dgate_ref[:, lanes] = (d_gated * mixed * (sig * (1.0 + gate * (1.0 - sig)))).astype(BF16)


def conv_back(d_conv, ci, masks, taps_ref, bufs, grads_ref, lanes):
    grads_ref[TAPS - 1 : TAPS, lanes] += jnp.sum(d_conv * ci, axis=0, keepdims=True)
    grads_ref[TAPS : TAPS + 1, lanes] += jnp.sum(d_conv, axis=0, keepdims=True)
    total = d_conv * taps_ref[TAPS - 1 : TAPS, lanes]
    for back in range(1, TAPS):
        tap = TAPS - 1 - back
        bufs[back - 1, :BLOCK, lanes] = d_conv * masks[back - 1]
        later = bufs[back - 1, back : back + BLOCK, lanes]
        grads_ref[tap : tap + 1, lanes] += jnp.sum(later * ci, axis=0, keepdims=True)
        total = total + taps_ref[tap : tap + 1, lanes] * later
    return total.astype(BF16)


def carry_rims(turn, bufs):
    @pl.when(turn == 0)
    def _():
        bufs[:, BLOCK:, :] = jnp.zeros((TAPS - 1, 8, bufs.shape[2]), F32)

    @pl.when(turn > 0)
    def _():
        bufs[:, BLOCK:, :] = bufs[:, :8, :]


def unmix_kernel(
    seqs, per, starts, place_ref, act_ref, step_ref, dmix_ref, y_ref, state_ref, slope_ref, ci_ref, taps_ref,
    skip_ref, bias_ref, decay_ref,
    dproj_ref, small_ref,
    carry, first, second, enter_full, xs_full, xw_full, spread_full, wide, bufs, grads_ref, heads_ref,
):
    turn = pl.program_id(0)
    turns = pl.num_programs(0)
    block = turns - 1 - turn
    cp = dmix_ref.shape[1]
    raw, step, rate, log_decay, cumulative, enter, leave, through = block_decays(
        starts, block, step_ref, bias_ref, decay_ref
    )

    @pl.when(turn == 0)
    def _():
        carry[...] = jnp.zeros_like(carry)
        wide[...] = jnp.zeros_like(wide)
        grads_ref[...] = jnp.zeros_like(grads_ref)
        heads_ref[...] = jnp.zeros_like(heads_ref)

    carry_rims(turn, bufs)
    state_in = act_ref[:, cp : cp + LANES]
    state_out = act_ref[:, cp + LANES : cp + 2 * LANES]
    scores_t = dot_nt(state_in, state_out)
    base = block * BLOCK
    rows = base + lax.broadcasted_iota(jnp.int32, (BLOCK, BLOCK), 0)
    cols = base + lax.broadcasted_iota(jnp.int32, (BLOCK, BLOCK), 1)
    allowed = (rows <= cols) & (doc_count(starts, rows) == doc_count(starts, cols))
    penalty = jnp.where(allowed, 0.0, FAR)
    place = base + lax.broadcasted_iota(jnp.int32, (BLOCK, LANES), 0)
    masks = [unbroken(starts, place, back) for back in range(1, TAPS)]
    scaled = cumulative * LOG2E
    cum_rows = jnp.transpose(scaled)
    state_out_t = jnp.transpose(state_out.astype(F32)).astype(BF16)
    left = lane_left(BLOCK)
    left_row = lane_left(1)
    for pair in range(cp // LANES):
        lanes = slice(pair * LANES, (pair + 1) * LANES)
        xs = (act_ref[:, lanes].astype(F32) * head_pair(step, pair, left)).astype(BF16)
        xs_full[:, lanes] = xs
        xw_full[:, lanes] = (xs.astype(F32) * head_pair(leave, pair, left)).astype(BF16)
        enter_full[:, lanes] = (dmix_ref[:, lanes].astype(F32) * head_pair(enter, pair, left)).astype(BF16)
    grad_b = carry[...].astype(BF16)
    d_out = dot_nt(enter_full[...], state_ref[0].astype(BF16))
    d_in = dot_nt(xw_full[...], grad_b)
    spread_full[...] = dot(state_in, grad_b)
    added = dot(state_out_t, enter_full[...])
    d_scores = [jnp.zeros((BLOCK // 2, BLOCK), F32), jnp.zeros((BLOCK // 2, BLOCK // 2), F32)]
    for pair in range(cp // LANES):
        lanes = slice(pair * LANES, (pair + 1) * LANES)
        x = act_ref[:, lanes].astype(F32)
        dmix = dmix_ref[:, lanes]
        dmix_f = dmix.astype(F32)
        xs_f = xs_full[:, lanes].astype(F32)
        spread = head_pair(leave, pair, left) * spread_full[:, lanes]
        pulled = None
        for side in range(2):
            head = 2 * pair + side
            mine = left if side == 0 else ~left
            xs_side = jnp.where(mine, xs_f, 0.0).astype(BF16)
            strips = []
            for index, (down, along) in enumerate(halves(True)):
                gaps = cum_rows[head : head + 1, along] - scaled[down, head : head + 1] + penalty[down, along]
                decay = jnp.exp2(gaps)
                mix = (scores_t[down, along] * decay).astype(BF16)
                strips.append(dot(mix, dmix[along, :]))
                d_scores[index] = d_scores[index] + dot_nt(xs_side[down, :], dmix[along, :]) * decay
            part = jnp.concatenate(strips, axis=0)
            pulled = part if side == 0 else jnp.where(left, pulled, part)
        pulled = pulled + spread
        dx = (head_pair(step, pair, left) * pulled + skip_ref[:, lanes] * dmix_f).astype(BF16)
        first[:, lanes] = dmix_f * y_ref[:, lanes] - xs_f * pulled
        second[:, lanes] = x * pulled
        grad = carry[:, lanes]
        through_b = head_pair(through, pair, left_row)
        wide[0:1, lanes] = jnp.sum(xs_f * spread, axis=0, keepdims=True) + through_b * jnp.sum(
            state_ref[0, :, lanes] * grad, axis=0, keepdims=True
        )
        wide[1:2, lanes] += jnp.sum(dmix_f * x, axis=0, keepdims=True)
        carry[:, lanes] = through_b * grad + added[:, lanes]
        d_conv = dx.astype(F32) * slope_ref[:, lanes].astype(F32)
        dproj_ref[:, lanes] = conv_back(
            d_conv, ci_ref[:, lanes].astype(F32), masks, taps_ref, bufs, grads_ref, lanes
        )

    half = BLOCK // 2
    d_scores_t = jnp.concatenate(
        [d_scores[0], jnp.concatenate([jnp.zeros((half, half), F32), d_scores[1]], axis=1)], axis=0
    )
    d_in = d_in + dot(d_scores_t.astype(BF16), state_out)
    d_out = d_out + dot(jnp.transpose(d_scores_t).astype(BF16), state_in)
    for part, at in ((d_in, cp), (d_out, cp + LANES)):
        lanes = slice(at, at + LANES)
        d_conv = part.astype(BF16).astype(F32) * slope_ref[:, lanes].astype(F32)
        dproj_ref[:, lanes] = conv_back(
            d_conv, ci_ref[:, lanes].astype(F32), masks, taps_ref, bufs, grads_ref, lanes
        )

    lane_head = lax.broadcasted_iota(jnp.int32, (cp, LANES), 0) // HEAD
    pick = jnp.where(lane_head == lax.broadcasted_iota(jnp.int32, (cp, LANES), 1), 1.0, 0.0).astype(BF16)
    d_cum = split_dot(pick, first[...], 2, True)
    d_step = split_dot(pick, second[...], 2, True)
    head_rows = split_dot(pick, wide[...], 3, True)
    upper = jnp.where(rows <= cols, 1.0, 0.0).astype(BF16)
    d_log = split_dot(upper, d_cum, 3) + head_rows[0:1, :]
    d_raw = (d_step + d_log * rate) * sigmoid(raw)
    dproj_ref[:, cp + 2 * LANES :] = d_raw.astype(BF16)
    heads_ref[0:1, :] += jnp.sum(d_log * log_decay, axis=0, keepdims=True)
    heads_ref[1:2, :] += jnp.sum(d_raw, axis=0, keepdims=True)
    heads_ref[2:3, :] = head_rows[1:2, :]

    @pl.when(turn == turns - 1)
    def _():
        owners = small_ref.shape[0]
        edge = LANES - per
        inner = per * owners - 2 * LANES
        cg = inner // seqs
        heads = cg // HEAD
        small_ref[...] = jnp.zeros_like(small_ref)
        for s in range(seqs):

            @pl.when(place_ref[0] == s)
            def _():
                for f in range(owners):
                    for low, high, base in ((s * cg, (s + 1) * cg, 0), (inner, per * owners, cp)):
                        a, b = max(low, f * per), min(high, (f + 1) * per)
                        if a < b:
                            small_ref[f, : TAPS + 1, edge + a - f * per : edge + b - f * per] = grads_ref[
                                : TAPS + 1, base + a - low : base + b - low
                            ]
                    small_ref[f, TAPS + 1 : TAPS + 4, edge + s * heads : edge + (s + 1) * heads] = heads_ref[
                        :3, :heads
                    ]


def back_kernel(dgate_ref, dproj_ref, w_ref, dn_ref):
    cp = dgate_ref.shape[1]
    dn_ref[...] = (dot_nt(dgate_ref[...], w_ref[:, :cp]) + dot_nt(dproj_ref[...], w_ref[:, cp:])).astype(BF16)


def call(kernel, name, micros, grid, ins, outs, scratch):
    def fixed(shape):
        return pl.BlockSpec(shape, lambda i: (0,) * len(shape))

    return pl.pallas_call(
        kernel,
        grid=(grid,),
        in_specs=[fixed(array.shape) if spec is None else spec for array, spec in ins],
        out_specs=[fixed(shape) if spec is None else spec for shape, _, spec in outs],
        out_shape=[jax.ShapeDtypeStruct(shape, kind) for shape, kind, _ in outs],
        scratch_shapes=[pltpu.VMEM(*kind) if isinstance(kind, tuple) else kind for kind in scratch],
        cost_estimate=pl.CostEstimate(
            flops=micros * 1000000000, bytes_accessed=micros * 3000000, transcendentals=0
        ),
        compiler_params=pltpu.CompilerParams(vmem_limit_bytes=VMEM_LIMIT),
        name=name,
    )(*[array for array, _ in ins])


SCALARS = pl.BlockSpec(memory_space=pltpu.SMEM)


def rows_spec(width, blocks, back=False):
    if back:
        return pl.BlockSpec((BLOCK, width), lambda i: (blocks - 1 - i, 0))
    return pl.BlockSpec((BLOCK, width), lambda i: (i, 0))


def pack_rows(seqs, place, in_weight, out_piece, taps, bias, norm, gain, states):
    shard, cg = out_piece.shape
    cp = -(-cg // LANES) * LANES
    return call(
        partial(pack_kernel, seqs),
        "pack",
        1,
        1,
        [(place, SCALARS)] + [(v, None) for v in (in_weight, out_piece, taps, bias, norm, gain)],
        [((shard, 3 * cp + states + LANES), BF16, None)],
        [((shard, LANES), F32)],
    )[0]


def halves_spec(seqs, blocks, width):
    if seqs == 2:
        return pl.BlockSpec((BLOCK, width), lambda i: (i % (blocks // 2), 0))
    return rows_spec(width, blocks)


def enter_rows(seqs, per, starts, place, places, mine, other, blocks, norm_row, weights, taps, length, cp, cc, inner):
    model = mine.shape[1]
    grid = length // BLOCK
    widths = [model, cp, cc, cc, cc, LANES]
    half = halves_spec(seqs, grid, model)
    outs = [((length, width), BF16, rows_spec(width, grid)) for width in widths]
    buf = ((BLOCK + 8, cc), F32)
    if not blocks:
        ins = [(starts, SCALARS), (place, SCALARS), (mine, half), (other, half)]
        ins = ins + [(norm_row, None), (weights, None), (taps, None)]
        return call(entry_kernel, "entry", 12, grid, ins, outs, [buf])
    count = len(blocks)
    anywhere = pl.BlockSpec(memory_space=pl.ANY)
    ins = [(starts, SCALARS), (places, SCALARS), (place, SCALARS), (mine, half), (other, half)]
    width = cp + cc + LANES
    return call(
        partial(first_entry_kernel, seqs, per, count),
        "entry",
        14,
        grid,
        ins + [(v, None) for v in blocks],
        outs
        + [
            ((model, width), BF16, anywhere),
            ((model, cp), BF16, anywhere),
            ((8, cc), F32, None),
            ((1, model), F32, None),
            ((1, cp), F32, None),
        ],
        [
            buf,
            ((model, width), BF16),
            ((model, cp), BF16),
            ((8, per * count), F32),
            ((1, inner), F32),
            pltpu.SemaphoreType.DMA((2,)),
        ],
    )


def mix_rows(seqs, starts, place, act, gate, step, mine, other, out_rows, gain_row, skip_row, bias_row, decay_row):
    length, cp = gate.shape
    model = mine.shape[1]
    blocks = length // BLOCK
    wide = rows_spec(cp, blocks)
    half = halves_spec(seqs, blocks, model)
    return call(
        mix_kernel,
        "mix",
        15,
        blocks,
        [
            (starts, SCALARS),
            (place, SCALARS),
            (act, rows_spec(act.shape[1], blocks)),
            (gate, wide),
            (step, rows_spec(LANES, blocks)),
            (mine, half),
            (other, half),
            (out_rows, None),
            (gain_row, None),
            (skip_row, None),
            (bias_row, None),
            (decay_row, None),
        ],
        [
            ((length, cp), F32, wide),
            ((length, cp), BF16, wide),
            ((length, cp), BF16, wide),
            ((length, model), BF16, rows_spec(model, blocks)),
            ((length, model), BF16, rows_spec(model, blocks)),
            ((8, length), F32, pl.BlockSpec((8, BLOCK), lambda i: (0, i))),
            ((blocks, LANES, cp), F32, pl.BlockSpec((1, LANES, cp), lambda i: (i, 0, 0))),
        ],
        [
            ((LANES, cp), F32),
            ((BLOCK, cp), F32),
            ((BLOCK, cp), F32),
            ((BLOCK, cp), BF16),
            ((BLOCK, cp), BF16),
        ],
    )


def ungate_rows(inner, stats, more, gate, mixed, dy, gain_row):
    length, cp = gate.shape
    blocks = length // BLOCK
    wide = rows_spec(cp, blocks)
    return call(
        partial(ungate_kernel, inner),
        "ungate",
        6,
        blocks,
        [(v, pl.BlockSpec((8, BLOCK), lambda i: (0, i))) for v in (stats, more)]
        + [(gate, wide), (mixed, wide), (dy, wide), (gain_row, None)],
        [((length, cp), BF16, wide)] * 3,
        [],
    )


def unmix_rows(
    seqs, per, owners, starts, place, act, step, dmix, y, states, slope, conv_in, taps, skip_row, bias_row, decay_row
):
    length, cp = dmix.shape
    cc = act.shape[1]
    blocks = length // BLOCK
    wide = rows_spec(cp, blocks, True)
    channels = rows_spec(cc, blocks, True)
    return call(
        partial(unmix_kernel, seqs, per),
        "unmix",
        28,
        blocks,
        [
            (starts, SCALARS),
            (place, SCALARS),
            (act, channels),
            (step, rows_spec(LANES, blocks, True)),
            (dmix, wide),
            (y, wide),
            (states, pl.BlockSpec((1, LANES, cp), lambda i: (blocks - 1 - i, 0, 0))),
            (slope, channels),
            (conv_in, channels),
            (taps, None),
            (skip_row, None),
            (bias_row, None),
            (decay_row, None),
        ],
        [
            ((length, cc + LANES), BF16, rows_spec(cc + LANES, blocks, True)),
            ((owners, 8, LANES), F32, None),
        ],
        [
            ((LANES, cp), F32),
            ((BLOCK, cp), F32),
            ((BLOCK, cp), F32),
            ((BLOCK, cp), BF16),
            ((BLOCK, cp), BF16),
            ((BLOCK, cp), BF16),
            ((BLOCK, cp), F32),
            ((8, cp), F32),
            ((TAPS - 1, BLOCK + 8, cc), F32),
            ((8, cc), F32),
            ((8, LANES), F32),
        ],
    )


def back_rows(part, parts, dgate, dproj, weights):
    length, cp = dgate.shape
    model = weights.shape[0]
    tall = 2 * BLOCK if parts == 2 else BLOCK
    blocks = length // parts // tall

    def at(i, part_ref):
        return (part_ref[0] * blocks + i, 0)

    return pl.pallas_call(
        lambda part_ref, *refs: back_kernel(*refs),
        grid_spec=pltpu.PrefetchScalarGridSpec(
            num_scalar_prefetch=1,
            grid=(blocks,),
            in_specs=[
                pl.BlockSpec((tall, cp), at),
                pl.BlockSpec((tall, dproj.shape[1]), at),
                pl.BlockSpec(weights.shape, lambda i, part_ref: (0, 0)),
            ],
            out_specs=pl.BlockSpec((tall, model), lambda i, part_ref: (i, 0)),
        ),
        out_shape=jax.ShapeDtypeStruct((length // parts, model), BF16),
        cost_estimate=pl.CostEstimate(flops=4000000000, bytes_accessed=12000000, transcendentals=0),
        compiler_params=pltpu.CompilerParams(vmem_limit_bytes=VMEM_LIMIT),
        name="back",
    )(part, dgate, dproj, weights)


def swap_bit(v, bit):
    count = lax.axis_size("fsdp")
    return lax.ppermute(v, "fsdp", [(i, i ^ (1 << bit)) for i in range(count)])


def halve(v, bits, left=None):
    count = lax.axis_size("fsdp").bit_length() - 1
    place = lax.axis_index("fsdp")
    left = list(range(count)) if left is None else list(left)
    for bit in bits:
        axis = len(left) - 1 - left.index(bit)
        left.remove(bit)
        mine = (place >> bit) & 1
        kept = lax.dynamic_index_in_dim(v, mine, axis, False)
        sent = lax.dynamic_index_in_dim(v, 1 - mine, axis, False)
        v = kept + swap_bit(sent, bit)
    return v


def by_bits(v):
    bits = v.shape[0].bit_length() - 1
    return v.reshape((2,) * bits + v.shape[1:])


def tied(*values):
    return lax.optimization_barrier(values)


class Ring:
    def __init__(self, v):
        count = lax.axis_size("fsdp")
        self.chips = count // 2
        place = lax.axis_index("fsdp")
        self.chip, self.core = place // 2, place % 2
        self.walk = list(range(0, self.chips, 2)) + list(range(1, self.chips, 2))[::-1]
        self.here = jnp.where(self.chip % 2 == 0, self.chip // 2, self.chips - 1 - self.chip // 2)
        self.up = self.down = v
        self.steps = 0
        self.found = []
        self.put(0, v)

    def chip_at(self, step):
        spot = (self.here + step) % self.chips
        return jnp.where(spot < (self.chips + 1) // 2, 2 * spot, 2 * (self.chips - 1 - spot) + 1)

    def turn(self, block, way):
        pairs = [
            (self.walk[i] * 2 + c, self.walk[(i + way) % self.chips] * 2 + c)
            for i in range(self.chips)
            for c in range(2)
        ]
        return lax.ppermute(block, "fsdp", pairs)

    def put(self, step, block):
        source = self.chip_at(step) * 2
        self.found.append((source + self.core, block))
        self.found.append((source + 1 - self.core, swap_bit(block, 0)))

    def step(self):
        self.steps += 1
        if 2 * self.steps < self.chips:
            self.up = self.turn(self.up, 1)
            self.down = self.turn(self.down, -1)
            self.put(-self.steps, self.up)
            self.put(self.steps, self.down)
        elif 2 * self.steps == self.chips:
            self.put(self.steps, self.turn(self.up, 1))

    def run(self, steps):
        for _ in range(steps):
            self.step()
        return self.found


def seq_swap(v):
    return lax.ppermute(v, "seq", [(0, 1), (1, 0)])


def seq_gather(v):
    if lax.axis_size("seq") != 2:
        return lax.all_gather(v, "seq", axis=0)
    other = seq_swap(v)
    low = lax.axis_index("seq") == 0
    return jnp.stack([jnp.where(low, v, other), jnp.where(low, other, v)])


def seq_scatter(v, axis):
    count = lax.axis_size("seq")
    if count != 2:
        return lax.psum_scatter(v, "seq", scatter_dimension=axis, tiled=True).astype(F32)
    place = lax.axis_index("seq")
    size = v.shape[axis] // 2
    sent = lax.dynamic_slice_in_dim(v, (1 - place) * size, size, axis)
    kept = lax.dynamic_slice_in_dim(v, place * size, size, axis)
    return kept.astype(F32) + seq_swap(sent).astype(F32)


def widen(v, width):
    if v.shape[-1] == width:
        return v
    return jnp.pad(v, [(0, 0)] * (v.ndim - 1) + [(0, width - v.shape[-1])])


def body(
    block_in,
    grad_out,
    doc_starts,
    in_weight,
    out_weight,
    conv_weight,
    conv_bias,
    norm_gain,
    gate_gain,
    decay_log,
    skip_gain,
    step_bias,
):
    seqs = lax.axis_size("seq")
    owners = lax.axis_size("fsdp")
    place = lax.axis_index("seq")
    rows_here, model = block_in.shape[1:]
    length = rows_here * seqs
    heads = decay_log.shape[0]
    heads_here = heads // seqs
    inner = out_weight.shape[0] * owners
    channels = conv_weight.shape[1] * owners
    states = channels - inner
    cg = heads_here * HEAD
    cp = -(-cg // LANES) * LANES
    cc = cp + states
    starts = doc_starts[0]

    shard, per = in_weight.shape[0], conv_bias.shape[0]
    place_row = place.reshape(1).astype(jnp.int32)
    out_piece = lax.dynamic_index_in_dim(out_weight.reshape(seqs, cg // owners, model), place, 0, False)
    out_piece = lax.ppermute(
        out_piece,
        ("seq", "fsdp"),
        [(s * owners + h, seqs * h + s) for s in range(seqs) for h in range(owners)],
    )
    own = pack_rows(
        seqs,
        place_row,
        in_weight,
        out_piece.reshape(shard, cg),
        conv_weight,
        conv_bias[None],
        norm_gain[None],
        gate_gain[None],
        states,
    )
    ring = Ring(own)
    if seqs == 2:
        tokens, others = block_in[0], seq_swap(block_in[0])
    else:
        tokens = others = lax.all_gather(block_in[0], "seq", axis=0, tiled=True)
    ring.run(min(2, owners // 4))
    grads = grad_out[0]
    ring.up, grads = tied(ring.up, grads)
    if seqs == 2:
        other_grads = seq_swap(grads)
    else:
        grads = other_grads = lax.all_gather(grads, "seq", axis=0, tiled=True)
    found = ring.run(owners // 4 - ring.steps)
    if cg == cp and cg // owners == shard and shard % 16 == 0:
        places = jnp.stack([spot for spot, _ in found])
        normed, gate, conv_in, act, slope, step, weights, out_rows, taps, norm_row, gain_row = enter_rows(
            seqs, per, starts, place_row, places, tokens, others, [v for _, v in found], None, None, None,
            length, cp, cc, inner,
        )
    else:
        gathered = jnp.zeros((owners,) + own.shape, BF16)
        for spot, v in found:
            gathered = lax.dynamic_update_index_in_dim(gathered, v, spot, 0)
        weights = gathered[:, :, : cp + cc + LANES].reshape(model, -1)
        out_rows = gathered[:, :, cp + cc + LANES : cp + cc + LANES + cg].reshape(cg, model)
        out_rows = jnp.pad(out_rows, ((0, cp - cg), (0, 0)))
        sides = gathered[:, :8, cp + cc + LANES - per : cp + cc + LANES].astype(F32)
        taps = sides.transpose(1, 0, 2).reshape(8, channels)
        taps = jnp.concatenate(
            [widen(lax.dynamic_slice_in_dim(taps, place * cg, cg, 1), cp), taps[:, inner:]], axis=1
        )
        norm_row = sides[:, TAPS + 1, :shard].reshape(1, model)
        gain_row = sides[:, TAPS + 2, : gate_gain.shape[0]].reshape(1, inner)
        gain_row = widen(lax.dynamic_slice_in_dim(gain_row, place * cg, cg, 1), cp)
        normed, gate, conv_in, act, slope, step = enter_rows(
            seqs, per, starts, place_row, None, tokens, others, None, norm_row, weights, taps, length, cp, cc, inner
        )

    def my_heads(v):
        return lax.dynamic_slice_in_dim(v, place * heads_here, heads_here)

    skip_row = widen(jnp.repeat(my_heads(skip_gain), HEAD)[None], cp)
    decay_row = widen(my_heads(decay_log)[None], LANES)
    step_row = widen(my_heads(step_bias)[None], LANES)

    y, mixed, dy, grads, partial_out, stats, states_kept = mix_rows(
        seqs, starts, place_row, act, gate, step, grads, other_grads, out_rows, gain_row, skip_row, step_row, decay_row
    )
    if seqs == 2:
        more = seq_swap(stats)
    else:
        stats, more = lax.psum(stats, "seq"), jnp.zeros_like(stats)
    out_sum = seq_scatter(partial_out, 0)
    squares = lax.dynamic_slice_in_dim(stats[0] + more[0], place * rows_here, rows_here)
    out_scale = lax.rsqrt(squares / inner + EPS)
    block_out = (block_in[0].astype(F32) + out_scale[:, None] * out_sum).astype(BF16)[None]

    bits = owners.bit_length() - 1
    dgate, dmix, gate_normed = ungate_rows(inner, stats, more, gate, mixed, dy, gain_row)
    early = by_bits(
        jnp.concatenate(
            [
                dot_tn(normed, dgate).astype(BF16).reshape(owners, shard, cp),
                dot_tn(gate_normed, grads).astype(BF16)[:cg].reshape(owners, shard, cg),
            ],
            axis=2,
        )
    )
    early = halve(early, [1])
    dproj, small_grads = unmix_rows(
        seqs, per, owners, starts, place_row, act, step, dmix, y, states_kept, slope, conv_in, taps,
        skip_row, step_row, decay_row,
    )
    dproj, early, out_sum = tied(dproj, early, out_sum)
    early = halve(early, [0], [0, *range(2, bits)])
    late = dot_tn(normed, dproj).astype(BF16).reshape(owners, shard, cc + LANES)
    late = late + jnp.pad(small_grads.astype(BF16), ((0, 0), (0, shard - 8), (cc, 0)))
    late = halve(by_bits(late), [0])
    late, early = tied(late, early)
    late = halve(late, [1], range(1, bits))
    early = halve(early, [2], range(2, bits))
    if seqs == 2:
        sent = back_rows(1 - place_row, 2, dgate, dproj, weights)
        kept = back_rows(place_row, 2, dgate, dproj, weights)
        got = seq_swap(sent)
    else:
        d_normed = back_rows(jnp.zeros_like(place_row), 1, dgate, dproj, weights)
        kept, got = lax.psum_scatter(d_normed, "seq", scatter_dimension=0, tiled=True), None
    kept, late, early = tied(kept, late, early)
    late = halve(late, [2], range(2, bits))
    early = halve(early, range(3, bits), range(3, bits))
    late = halve(late, range(3, bits), range(3, bits))
    if got is not None:
        late, got = tied(late, got)
    late, early = tied(late, early)
    late_all = seq_gather(jnp.concatenate([early[:, :cp], late], axis=1)).astype(F32)
    piece = early[:, cp:].reshape(cg // owners, model)
    found = []
    for turn in range(seqs):
        pairs = []
        for q in range(seqs * owners):
            pairs.append((q, ((q + turn) % seqs) * owners + q // seqs))
        found.append(lax.ppermute(piece, ("seq", "fsdp"), pairs))
    d_normed_mine = kept.astype(F32)
    if got is not None:
        d_normed_mine = d_normed_mine + got.astype(F32)

    early_all, late_all = late_all[:, :, :cg], late_all[:, :, cp:]

    def columns(v):
        return jnp.concatenate([v[i] for i in range(seqs)], axis=1)

    in_grad = jnp.concatenate(
        [
            columns(early_all),
            columns(late_all[:, :, :cg]),
            jnp.sum(late_all[:, :, cp:cc], axis=0),
            columns(late_all[:, :, cc : cc + heads_here]),
        ],
        axis=1,
    )
    norm_grad = jnp.sum(in_grad * in_weight.astype(F32), axis=1) / norm_gain.astype(F32)
    small_sums = jnp.sum(late_all[:, :8, cc + LANES - per :], axis=0)
    head_out = small_sums[TAPS + 1 : TAPS + 4, :heads]

    found = jnp.stack(found)
    out_grad = jnp.concatenate(
        [lax.dynamic_index_in_dim(found, (place - i) % seqs, 0, False) for i in range(seqs)], axis=0
    ).astype(F32)
    gain_grad = jnp.sum(out_grad * out_weight.astype(F32), axis=1) / gate_gain.astype(F32)

    x = block_in[0].astype(F32)
    scale = lax.rsqrt(jnp.mean(x * x, axis=-1, keepdims=True) + EPS)
    gained = d_normed_mine * norm_row
    along = scale * scale * jnp.mean(gained * x, axis=-1, keepdims=True)
    grad_in = (grad_out[0].astype(F32) + scale * (gained - x * along)).astype(BF16)[None]

    return (
        block_out,
        grad_in,
        in_grad,
        out_grad,
        small_sums[:TAPS],
        small_sums[TAPS],
        norm_grad,
        gain_grad,
        head_out[0],
        head_out[2],
        head_out[1],
    )


def solution(mesh):
    placed = (
        P("fsdp", "seq", None),
        P("fsdp", "seq", None),
        P("fsdp", None),
        P("fsdp", None),
        P("fsdp", None),
        P(None, "fsdp"),
        P("fsdp"),
        P("fsdp"),
        P("fsdp"),
        P(),
        P(),
        P(),
    )
    return jax.shard_map(
        body,
        mesh=mesh,
        in_specs=placed,
        out_specs=(
            P("fsdp", "seq", None),
            P("fsdp", "seq", None),
            P("fsdp", None),
            P("fsdp", None),
            P(None, "fsdp"),
            P("fsdp"),
            P("fsdp"),
            P("fsdp"),
            P(),
            P(),
            P(),
        ),
        check_vma=False,
    )
```

```python
from functools import partial

import jax
import jax.numpy as jnp
from jax import lax
from jax.experimental import pallas as pl
from jax.experimental.pallas import tpu as pltpu
from jax.sharding import PartitionSpec as P

BLOCK = 256
LANES = 128
HEAD = 64
TAPS = 4
EPS = 1e-05
FAR = -1e30
LOG2E = 1.4426950408889634
VMEM_LIMIT = 22 * 1024 * 1024
F32 = jnp.float32
BF16 = jnp.bfloat16


def dot(a, b):
    return jnp.dot(a, b, preferred_element_type=F32)


def dot_nt(a, b):
    return lax.dot_general(a, b, (((1,), (1,)), ((), ())), preferred_element_type=F32)


def dot_tn(a, b):
    return lax.dot_general(a, b, (((0,), (0,)), ((), ())), preferred_element_type=F32)


def split_dot(product, left, values, parts):
    total = None
    rest = values
    for _ in range(parts):
        term = rest.astype(BF16)
        rest = rest - term.astype(F32)
        piece = product(left, term)
        total = piece if total is None else total + piece
    return total


def sigmoid(v):
    return 0.5 + 0.5 * jnp.tanh(0.5 * v)


def softplus(v):
    t = jnp.exp(-jnp.abs(v))
    small = t * (1.0 - t * (0.5 - t * (1.0 / 3.0 - t * 0.25)))
    return jnp.maximum(v, 0.0) + jnp.where(t < 0.01, small, jnp.log(1.0 + t))


def doc_count(starts, place):
    total = (place >= starts[0]).astype(jnp.int32)
    for k in range(1, starts.shape[0]):
        total = total + (place >= starts[k]).astype(jnp.int32)
    return total


def doc_masks(starts, place, ahead):
    edge = jnp.full(place.shape, 2**30 if ahead else 0, jnp.int32)
    for k in range(starts.shape[0]):
        if ahead:
            edge = jnp.minimum(edge, jnp.where(starts[k] > place, starts[k], 2**30))
        else:
            edge = jnp.maximum(edge, jnp.where(starts[k] <= place, starts[k], 0))
    room = edge - place - 1 if ahead else place - edge
    return [jnp.where(room >= back, 1.0, 0.0) for back in range(1, TAPS)]


def head_pair(values, pair, left):
    return jnp.where(left, values[:, 2 * pair : 2 * pair + 1], values[:, 2 * pair + 1 : 2 * pair + 2])


def head_column(values, head):
    return jnp.broadcast_to(values[:, head : head + 1], (values.shape[0], LANES))


def lane_left(rows):
    return lax.broadcasted_iota(jnp.int32, (rows, LANES), 1) < HEAD


def pack_kernel(
    seqs, place_ref, in_ref, out_ref, taps_ref, bias_ref, norm_ref, gain_ref, own_ref, tile
):
    cg, per = out_ref.shape[1], taps_ref.shape[1]
    cp = -(-cg // LANES) * LANES
    inner = cg * seqs
    heads = cg // HEAD
    states = own_ref.shape[1] - 3 * cp - LANES
    if cp != cg:
        own_ref[...] = jnp.zeros_like(own_ref)
    tile[...] = jnp.zeros_like(tile)
    at = 2 * inner + states
    for s in range(seqs):

        @pl.when(place_ref[0] == s)
        def _():
            own_ref[:, :cg] = in_ref[:, s * cg : (s + 1) * cg]
            own_ref[:, cp : cp + cg] = in_ref[:, inner + s * cg : inner + (s + 1) * cg]
            tile[:, :heads] = in_ref[:, at + s * heads : at + (s + 1) * heads].astype(F32)

    own_ref[:, 2 * cp : 2 * cp + states] = in_ref[:, 2 * inner : at]
    tile[:TAPS, LANES - per :] = taps_ref[...].astype(F32)
    tile[TAPS : TAPS + 1, LANES - per :] = bias_ref[...].astype(F32)
    tile[TAPS + 1 : TAPS + 2, LANES - per : LANES - per + norm_ref.shape[1]] = norm_ref[...].astype(F32)
    tile[TAPS + 2 : TAPS + 3, LANES - per : LANES - per + gain_ref.shape[1]] = gain_ref[...].astype(F32)
    own_ref[:, 2 * cp + states : 2 * cp + states + LANES] = tile[...].astype(BF16)
    own_ref[:, 2 * cp + states + LANES : 2 * cp + states + LANES + cg] = out_ref[...]


def assemble(
    seqs, per, places, place_ref, blocks, w_ref, wo_ref, taps_ref, norm_ref, gain_ref, taps_all, gain_all, sems
):
    count = len(blocks)
    shard = blocks[0].shape[0]
    width = w_ref.shape[1]
    copies = []
    for k, block in enumerate(blocks):
        rows = pl.ds(pl.multiple_of(places[k] * shard, 16), shard)
        copies.append(pltpu.make_async_copy(block.at[:, :width], w_ref.at[rows, :], sems.at[2 * k]))
        copies.append(pltpu.make_async_copy(block.at[:, width:], wo_ref.at[rows, :], sems.at[2 * k + 1]))
    for copy in copies:
        copy.start()
    for copy in copies:
        copy.wait()
    some = gain_all.shape[1] // count
    for f in range(count):
        side = w_ref[f * shard : f * shard + 16, width - LANES :].astype(F32)[:, LANES - per :]
        taps_all[:8, f * per : (f + 1) * per] = side[:8, :]
        norm_ref[:, f * shard : (f + 1) * shard] = side[TAPS + 1 : TAPS + 2, :shard]
        gain_all[:, f * some : (f + 1) * some] = side[TAPS + 2 : TAPS + 3, :some]
    cp = gain_ref.shape[1]
    taps_ref[:, cp:] = taps_all[:, cp * seqs :]
    for s in range(seqs):

        @pl.when(place_ref[0] == s)
        def _():
            taps_ref[:, :cp] = taps_all[:, s * cp : (s + 1) * cp]
            gain_ref[...] = gain_all[:, s * cp : (s + 1) * cp]


def first_entry_kernel(seqs, per, count, starts, places, place_ref, mine_ref, other_ref, *refs):
    blocks = refs[:count]
    outs, (w_out, wo_out, taps_ref, norm_ref, gain_ref) = refs[count : count + 6], refs[count + 6 : count + 11]
    buf, w_ref, wo_ref, taps_all, gain_all, sems, sems_in = refs[count + 11 :]
    copies = [
        pltpu.make_async_copy(w_ref, w_out, sems.at[0]),
        pltpu.make_async_copy(wo_ref, wo_out, sems.at[1]),
    ]

    @pl.when(pl.program_id(0) == 0)
    def _():
        assemble(
            seqs, per, places, place_ref, blocks, w_ref, wo_ref, taps_ref, norm_ref, gain_ref, taps_all, gain_all, sems_in
        )
        for copy in copies:
            copy.start()

    entry_kernel(starts, place_ref, mine_ref, other_ref, norm_ref, w_ref, taps_ref, *outs, buf)

    @pl.when(pl.program_id(0) == pl.num_programs(0) - 1)
    def _():
        for copy in copies:
            copy.wait()


def row_block(place_ref, block, mine_ref, other_ref):
    mine = 2 * block // pl.num_programs(0) == place_ref[0]
    return jnp.where(mine, mine_ref[...].astype(F32), other_ref[...].astype(F32))


def entry_kernel(
    starts, place_ref, mine_ref, other_ref, norm_ref, w_ref, taps_ref,
    xn_ref, gate_ref, ci_ref, act_ref, slope_ref, step_ref, buf,
):
    block = pl.program_id(0)
    cp = gate_ref.shape[1]
    cc = act_ref.shape[1]
    x = row_block(place_ref, block, mine_ref, other_ref)
    scale = lax.rsqrt(jnp.mean(x * x, axis=-1, keepdims=True) + EPS)
    xn = (x * scale * norm_ref[...]).astype(BF16)
    xn_ref[...] = xn
    gate_ref[...] = dot(xn, w_ref[:, :cp]).astype(BF16)
    step = dot(xn, w_ref[:, cp + cc :]).astype(BF16).astype(F32)
    step_ref[...] = jnp.transpose(step)[: step_ref.shape[0], :]

    @pl.when(block == 0)
    def _():
        buf[:, :8, :] = jnp.zeros((cc // LANES, 8, LANES), F32)

    @pl.when(block > 0)
    def _():
        buf[:, :8, :] = buf[:, BLOCK : BLOCK + 8, :]

    ci = dot(xn, w_ref[:, cp : cp + cc]).astype(BF16)
    ci_ref[...] = ci
    place = block * BLOCK + lax.broadcasted_iota(jnp.int32, (BLOCK, LANES), 0)
    masks = doc_masks(starts, place, False)
    for tile in range(cc // LANES):
        cols = slice(tile * LANES, (tile + 1) * LANES)
        here = ci[:, cols].astype(F32)
        buf[tile, 8:, :] = here
        total = taps_ref[TAPS : TAPS + 1, cols] + taps_ref[TAPS - 1 : TAPS, cols] * here
        for back in range(1, TAPS):
            tap = taps_ref[TAPS - 1 - back : TAPS - back, cols]
            total = total + masks[back - 1] * tap * buf[tile, 8 - back : 8 - back + BLOCK, :]
        sig = sigmoid(total)
        act_ref[:, cols] = (total * sig).astype(BF16)
        slope_ref[:, cols] = (sig * (1.0 + total * (1.0 - sig))).astype(BF16)


def tri(upper):
    rows = lax.broadcasted_iota(jnp.int32, (BLOCK, BLOCK), 0)
    cols = lax.broadcasted_iota(jnp.int32, (BLOCK, BLOCK), 1)
    return rows <= cols if upper else rows >= cols


def as_columns(*rows):
    stack = jnp.concatenate(rows, axis=0)
    rest = LANES - stack.shape[0]
    return jnp.transpose(jnp.concatenate([stack, jnp.zeros((rest, BLOCK), F32)], axis=0))


def block_decays(starts, block, step_ref, bias_ref, decay_ref):
    raw = step_ref[...] + bias_ref[...]
    step = softplus(raw)
    rate = -jnp.exp(decay_ref[...])
    log_decay = rate * step
    ones = jnp.where(tri(True), 1.0, 0.0).astype(BF16)
    running = split_dot(lambda m, v: dot(v, m), ones, log_decay * LOG2E, 3)
    return raw, step, rate, log_decay, running


def block_docs(starts, block, upper):
    base = block * BLOCK
    place = base + lax.broadcasted_iota(jnp.int32, (BLOCK, LANES), 0)
    docs = doc_count(starts, place)
    docs_row = doc_count(starts, base + lax.broadcasted_iota(jnp.int32, (1, BLOCK), 1))
    prev = doc_count(starts, base - 1)
    last = doc_count(starts, base + BLOCK - 1)
    docs_wide = jnp.concatenate([docs] * (BLOCK // LANES), axis=1)
    penalty = jnp.where(tri(upper) & (docs_wide == docs_row), 0.0, FAR)
    enter = jnp.where(docs == prev, 0.0, FAR)
    leave = jnp.where(docs == last, 0.0, FAR)
    return place, penalty, enter, leave, jnp.where(last == prev, 1.0, 0.0)


def halves(upper):
    half = BLOCK // 2
    if upper:
        return [(slice(0, half), slice(0, BLOCK)), (slice(half, BLOCK), slice(half, BLOCK))]
    return [(slice(0, half), slice(0, half)), (slice(half, BLOCK), slice(0, BLOCK))]


def wide_column(column, down, along):
    return jnp.concatenate([column[down, :]] * ((along.stop - along.start) // LANES), axis=1)


def mix_kernel(
    starts, place_ref, act_ref, gate_ref, step_ref, mine_ref, other_ref, wout_ref, gain_ref, skip_ref, bias_ref,
    decay_ref,
    y_ref, mixed_ref, dy_ref, g_ref, u_ref, stats_ref, state_ref, carry, from_state, dy_full, xw_full, gated_full,
):
    block = pl.program_id(0)
    cp = gate_ref.shape[1]
    raw, step, rate, log_decay, running = block_decays(starts, block, step_ref, bias_ref, decay_ref)
    place, penalty, enter, leave, through = block_docs(starts, block, False)
    many = step.shape[0]
    columns = as_columns(running, step)
    final = columns[BLOCK - 1 : BLOCK, :]

    @pl.when(block == 0)
    def _():
        carry[...] = jnp.zeros_like(carry)

    state_ref[0] = carry[...]
    state_in = act_ref[:, cp : cp + LANES]
    state_out = act_ref[:, cp + LANES : cp + 2 * LANES]
    scores = dot_nt(state_out, state_in)
    from_state[...] = dot(state_out, carry[...].astype(BF16))
    grad = row_block(place_ref, block, mine_ref, other_ref).astype(BF16)
    g_ref[...] = grad
    dy_full[...] = dot_nt(grad, wout_ref[...])
    left = lane_left(BLOCK)
    left_row = lane_left(1)
    squares = jnp.zeros((BLOCK, LANES), F32)
    crosses = jnp.zeros((BLOCK, LANES), F32)
    for pair in range(cp // LANES):
        lanes = slice(pair * LANES, (pair + 1) * LANES)
        x = act_ref[:, lanes].astype(F32)
        xs = (x * jnp.where(left, head_column(columns, many + 2 * pair), head_column(columns, many + 2 * pair + 1))).astype(BF16)
        sums = [head_column(columns, 2 * pair), head_column(columns, 2 * pair + 1)]
        both = jnp.where(left, sums[0], sums[1])
        within = None
        for side in range(2):
            head = 2 * pair + side
            strips = []
            for down, along in halves(False):
                gaps = wide_column(sums[side], down, along) - running[head : head + 1, along] + penalty[down, along]
                mix = (scores[down, along] * jnp.exp2(gaps)).astype(BF16)
                strips.append(dot(mix, xs[along, :]))
            part = jnp.concatenate(strips, axis=0)
            within = part if side == 0 else jnp.where(left, within, part)
        y = within + jnp.exp2(both + enter) * from_state[:, lanes]
        y_ref[:, lanes] = y
        xw_full[:, lanes] = (xs.astype(F32) * jnp.exp2(head_pair(final, pair, left_row) - both + leave)).astype(BF16)
        mixed = (y + skip_ref[:, lanes] * x).astype(BF16)
        mixed_ref[:, lanes] = mixed
        gate = gate_ref[:, lanes].astype(F32)
        gated = mixed.astype(F32) * gate * sigmoid(gate)
        dy = dy_full[:, lanes]
        dy_ref[:, lanes] = dy.astype(BF16)
        gained = gated * gain_ref[:, lanes]
        squares = squares + gated * gated
        crosses = crosses + dy * gained
        gated_full[:, lanes] = gained.astype(BF16)
    state_in_t = jnp.transpose(state_in.astype(F32)).astype(BF16)
    added = dot(state_in_t, xw_full[...])
    for pair in range(cp // LANES):
        lanes = slice(pair * LANES, (pair + 1) * LANES)
        kept = through * jnp.exp2(head_pair(final, pair, left_row))
        carry[:, lanes] = kept * carry[:, lanes] + added[:, lanes]
    u_ref[...] = dot(gated_full[...], wout_ref[...]).astype(BF16)
    lane = lax.broadcasted_iota(jnp.int32, (BLOCK, LANES), 1)
    sums = jnp.where(lane == 0, jnp.sum(squares, axis=1, keepdims=True), 0.0) + jnp.where(
        lane == 1, jnp.sum(crosses, axis=1, keepdims=True), 0.0
    )
    stats_ref[...] = jnp.transpose(sums)[:8, :]


def ungate_kernel(inner, stats_ref, more_ref, gate_ref, mixed_ref, dy_ref, gain_ref, dgate_ref, dmix_ref, gn_ref):
    cp = gate_ref.shape[1]
    stats = stats_ref[...] + more_ref[...]
    stats = jnp.transpose(jnp.concatenate([stats, jnp.zeros((LANES - 8, BLOCK), F32)], axis=0))
    scale = lax.rsqrt(stats[:, 0:1] / inner + EPS)
    pull = scale * scale * scale * stats[:, 1:2] / inner
    for pair in range(cp // LANES):
        lanes = slice(pair * LANES, (pair + 1) * LANES)
        gate = gate_ref[:, lanes].astype(F32)
        mixed = mixed_ref[:, lanes].astype(F32)
        sig = sigmoid(gate)
        silu = gate * sig
        gated = mixed * silu
        gain = gain_ref[:, lanes]
        gn_ref[:, lanes] = (gated * scale * gain).astype(BF16)
        d_gated = scale * gain * dy_ref[:, lanes].astype(F32) - gated * pull
        dmix_ref[:, lanes] = (d_gated * silu).astype(BF16)
        dgate_ref[:, lanes] = (d_gated * mixed * (sig * (1.0 + gate * (1.0 - sig)))).astype(BF16)


def tall_sum(v):
    return jnp.sum(v.reshape(v.shape[0] // 8, 8, v.shape[1]), axis=0)


def conv_back(d_conv, ci, masks, taps_ref, buf, sums, tile):
    lanes = slice(tile * LANES, (tile + 1) * LANES)
    sums[TAPS - 1, :, lanes] += tall_sum(d_conv * ci)
    sums[TAPS, :, lanes] += tall_sum(d_conv)
    total = d_conv * taps_ref[TAPS - 1 : TAPS, lanes]
    buf[tile, :BLOCK, :] = d_conv
    for back in range(1, TAPS):
        tap = TAPS - 1 - back
        later = buf[tile, back : back + BLOCK, :] * masks[back - 1]
        sums[tap, :, lanes] += tall_sum(later * ci)
        total = total + taps_ref[tap : tap + 1, lanes] * later
    return total.astype(BF16)


def carry_rims(turn, buf):
    @pl.when(turn == 0)
    def _():
        buf[:, BLOCK:, :] = jnp.zeros((buf.shape[0], 8, LANES), F32)

    @pl.when(turn > 0)
    def _():
        buf[:, BLOCK:, :] = buf[:, :8, :]


def unmix_kernel(
    seqs, per, starts, place_ref, act_ref, step_ref, dmix_ref, y_ref, state_ref, slope_ref, ci_ref, taps_ref,
    skip_ref, bias_ref, decay_ref,
    dproj_ref, small_ref,
    carry, first, second, enter_full, xs_full, xw_full, spread_full, step_full, leave_full, wide, buf, sums,
    skips, decays, biases,
):
    turn = pl.program_id(0)
    turns = pl.num_programs(0)
    block = turns - 1 - turn
    cp = dmix_ref.shape[1]
    raw, step, rate, log_decay, running = block_decays(starts, block, step_ref, bias_ref, decay_ref)
    place, penalty, enter, leave, through = block_docs(starts, block, True)
    many = step.shape[0]
    columns = as_columns(running, step)
    final = columns[BLOCK - 1 : BLOCK, :]

    @pl.when(turn == 0)
    def _():
        carry[...] = jnp.zeros_like(carry)
        sums[...] = jnp.zeros_like(sums)
        skips[...] = jnp.zeros_like(skips)
        decays[...] = jnp.zeros_like(decays)
        biases[...] = jnp.zeros_like(biases)

    carry_rims(turn, buf)
    state_in = act_ref[:, cp : cp + LANES]
    state_out = act_ref[:, cp + LANES : cp + 2 * LANES]
    scores_t = dot_nt(state_in, state_out)
    masks = doc_masks(starts, place, True)
    state_out_t = jnp.transpose(state_out.astype(F32)).astype(BF16)
    left = lane_left(BLOCK)
    left_row = lane_left(1)
    for pair in range(cp // LANES):
        lanes = slice(pair * LANES, (pair + 1) * LANES)
        step_b = jnp.where(left, head_column(columns, many + 2 * pair), head_column(columns, many + 2 * pair + 1))
        both = jnp.where(left, head_column(columns, 2 * pair), head_column(columns, 2 * pair + 1))
        leave_b = jnp.exp2(head_pair(final, pair, left_row) - both + leave)
        step_full[:, lanes] = step_b
        leave_full[:, lanes] = leave_b
        xs = (act_ref[:, lanes].astype(F32) * step_b).astype(BF16)
        xs_full[:, lanes] = xs
        xw_full[:, lanes] = (xs.astype(F32) * leave_b).astype(BF16)
        enter_full[:, lanes] = (dmix_ref[:, lanes].astype(F32) * jnp.exp2(both + enter)).astype(BF16)
    grad_b = carry[...].astype(BF16)
    d_out = dot_nt(enter_full[...], state_ref[0].astype(BF16))
    d_in = dot_nt(xw_full[...], grad_b)
    spread_full[...] = dot(state_in, grad_b)
    added = dot(state_out_t, enter_full[...])
    d_scores = [jnp.zeros((BLOCK // 2, BLOCK), F32), jnp.zeros((BLOCK // 2, BLOCK // 2), F32)]
    for pair in range(cp // LANES):
        lanes = slice(pair * LANES, (pair + 1) * LANES)
        x = act_ref[:, lanes].astype(F32)
        dmix = dmix_ref[:, lanes]
        dmix_f = dmix.astype(F32)
        xs_f = xs_full[:, lanes].astype(F32)
        spread = leave_full[:, lanes] * spread_full[:, lanes]
        pulled = None
        for side in range(2):
            head = 2 * pair + side
            mine = left if side == 0 else ~left
            xs_side = jnp.where(mine, xs_f, 0.0).astype(BF16)
            strips = []
            column = head_column(columns, head)
            for index, (down, along) in enumerate(halves(True)):
                gaps = running[head : head + 1, along] - wide_column(column, down, along) + penalty[down, along]
                decay = jnp.exp2(gaps)
                mix = (scores_t[down, along] * decay).astype(BF16)
                strips.append(dot(mix, dmix[along, :]))
                d_scores[index] = d_scores[index] + dot_nt(xs_side[down, :], dmix[along, :]) * decay
            part = jnp.concatenate(strips, axis=0)
            pulled = part if side == 0 else jnp.where(left, pulled, part)
        pulled = pulled + spread
        dx = (step_full[:, lanes] * pulled + skip_ref[:, lanes] * dmix_f).astype(BF16)
        first[:, lanes] = dmix_f * y_ref[:, lanes] - xs_f * pulled
        second[:, lanes] = x * pulled
        grad = carry[:, lanes]
        through_b = through * jnp.exp2(head_pair(final, pair, left_row))
        wide[:, lanes] = tall_sum(xs_f * spread) + through_b * tall_sum(state_ref[0, :, lanes] * grad)
        skips[:, lanes] += tall_sum(dmix_f * x)
        carry[:, lanes] = through_b * grad + added[:, lanes]
        d_conv = dx.astype(F32) * slope_ref[:, lanes].astype(F32)
        dproj_ref[:, lanes] = conv_back(d_conv, ci_ref[:, lanes].astype(F32), masks, taps_ref, buf, sums, pair)

    half = BLOCK // 2
    d_scores_t = jnp.concatenate(
        [d_scores[0], jnp.concatenate([jnp.zeros((half, half), F32), d_scores[1]], axis=1)], axis=0
    )
    d_in = d_in + dot(d_scores_t.astype(BF16), state_out)
    d_out = d_out + dot(jnp.transpose(d_scores_t).astype(BF16), state_in)
    for part, at in ((d_in, cp), (d_out, cp + LANES)):
        lanes = slice(at, at + LANES)
        d_conv = part.astype(BF16).astype(F32) * slope_ref[:, lanes].astype(F32)
        dproj_ref[:, lanes] = conv_back(
            d_conv, ci_ref[:, lanes].astype(F32), masks, taps_ref, buf, sums, at // LANES
        )

    head_of = lax.broadcasted_iota(jnp.int32, (many, cp), 1) // HEAD
    pick = jnp.where(head_of == lax.broadcasted_iota(jnp.int32, (many, cp), 0), 1.0, 0.0).astype(BF16)
    d_cum = split_dot(dot_nt, pick, first[...], 2)
    d_step = split_dot(dot_nt, pick, second[...], 2)
    d_final = jnp.sum(split_dot(dot_nt, pick, wide[...], 3), axis=1, keepdims=True)
    ones = jnp.where(tri(False), 1.0, 0.0).astype(BF16)
    d_log = split_dot(lambda m, v: dot(v, m), ones, d_cum, 3) + d_final
    d_raw = (d_step + d_log * rate) * sigmoid(raw)
    dproj_ref[:, cp + 2 * LANES :] = as_columns(d_raw).astype(BF16)
    decays[...] += d_log * log_decay
    biases[...] += d_raw

    @pl.when(turn == turns - 1)
    def _():
        owners = small_ref.shape[0]
        edge = LANES - per
        inner = per * owners - 2 * LANES
        cg = inner // seqs
        heads = cg // HEAD
        small_ref[...] = jnp.zeros_like(small_ref)
        skip_sums = split_dot(lambda m, v: dot_nt(v, m), pick, skips[...], 3)
        head_rows = [
            jnp.sum(as_columns(decays[...]), axis=0, keepdims=True),
            jnp.sum(as_columns(biases[...]), axis=0, keepdims=True),
            jnp.sum(skip_sums, axis=0, keepdims=True),
        ]
        grads = jnp.concatenate([jnp.sum(sums[k], axis=0, keepdims=True) for k in range(TAPS + 1)], axis=0)
        for s in range(seqs):

            @pl.when(place_ref[0] == s)
            def _():
                for f in range(owners):
                    for low, high, base in ((s * cg, (s + 1) * cg, 0), (inner, per * owners, cp)):
                        a, b = max(low, f * per), min(high, (f + 1) * per)
                        if a < b:
                            small_ref[f, : TAPS + 1, edge + a - f * per : edge + b - f * per] = grads[
                                :, base + a - low : base + b - low
                            ]
                    for k, row in enumerate(head_rows):
                        small_ref[f, TAPS + 1 + k : TAPS + 2 + k, edge + s * heads : edge + (s + 1) * heads] = row[
                            :, :heads
                        ]


def back_kernel(dgate_ref, dproj_ref, w_ref, dn_ref):
    cp = dgate_ref.shape[1]
    dn_ref[...] = (dot_nt(dgate_ref[...], w_ref[:, :cp]) + dot_nt(dproj_ref[...], w_ref[:, cp:])).astype(BF16)


def call(kernel, name, micros, grid, ins, outs, scratch):
    def fixed(shape):
        return pl.BlockSpec(shape, lambda i: (0,) * len(shape))

    return pl.pallas_call(
        kernel,
        grid=(grid,),
        in_specs=[fixed(array.shape) if spec is None else spec for array, spec in ins],
        out_specs=[fixed(shape) if spec is None else spec for shape, _, spec in outs],
        out_shape=[jax.ShapeDtypeStruct(shape, kind) for shape, kind, _ in outs],
        scratch_shapes=[pltpu.VMEM(*kind) if isinstance(kind, tuple) else kind for kind in scratch],
        cost_estimate=pl.CostEstimate(
            flops=micros * 1000000000, bytes_accessed=micros * 3000000, transcendentals=0
        ),
        compiler_params=pltpu.CompilerParams(vmem_limit_bytes=VMEM_LIMIT),
        name=name,
    )(*[array for array, _ in ins])


SCALARS = pl.BlockSpec(memory_space=pltpu.SMEM)


def rows_spec(width, blocks, back=False):
    if back:
        return pl.BlockSpec((BLOCK, width), lambda i: (blocks - 1 - i, 0))
    return pl.BlockSpec((BLOCK, width), lambda i: (i, 0))


def pack_rows(seqs, place, in_weight, out_piece, taps, bias, norm, gain, states):
    shard, cg = out_piece.shape
    cp = -(-cg // LANES) * LANES
    return call(
        partial(pack_kernel, seqs),
        "pack",
        1,
        1,
        [(place, SCALARS)] + [(v, None) for v in (in_weight, out_piece, taps, bias, norm, gain)],
        [((shard, 3 * cp + states + LANES), BF16, None)],
        [((shard, LANES), F32)],
    )[0]


def halves_spec(seqs, blocks, width):
    if seqs == 2:
        return pl.BlockSpec((BLOCK, width), lambda i: (i % (blocks // 2), 0))
    return rows_spec(width, blocks)


def enter_rows(seqs, per, starts, place, places, mine, other, blocks, norm_row, weights, taps, length, cp, cc, inner):
    model = mine.shape[1]
    grid = length // BLOCK
    widths = [model, cp, cc, cc, cc]
    many = -(-(cp // HEAD) // 8) * 8
    half = halves_spec(seqs, grid, model)
    outs = [((length, width), BF16, rows_spec(width, grid)) for width in widths]
    outs.append(((many, length), F32, pl.BlockSpec((many, BLOCK), lambda i: (0, i))))
    buf = ((cc // LANES, BLOCK + 8, LANES), F32)
    if not blocks:
        ins = [(starts, SCALARS), (place, SCALARS), (mine, half), (other, half)]
        ins = ins + [(norm_row, None), (weights, None), (taps, None)]
        return call(entry_kernel, "entry", 12, grid, ins, outs, [buf])
    count = len(blocks)
    anywhere = pl.BlockSpec(memory_space=pl.ANY)
    ins = [(starts, SCALARS), (places, SCALARS), (place, SCALARS), (mine, half), (other, half)]
    width = cp + cc + LANES
    return call(
        partial(first_entry_kernel, seqs, per, count),
        "entry",
        14,
        grid,
        ins + [(v, anywhere) for v in blocks],
        outs
        + [
            ((model, width), BF16, anywhere),
            ((model, cp), BF16, anywhere),
            ((8, cc), F32, None),
            ((1, model), F32, None),
            ((1, cp), F32, None),
        ],
        [
            buf,
            ((model, width), BF16),
            ((model, cp), BF16),
            ((8, per * count), F32),
            ((1, inner), F32),
            pltpu.SemaphoreType.DMA((2,)),
            pltpu.SemaphoreType.DMA((2 * count,)),
        ],
    )


def mix_rows(seqs, starts, place, act, gate, step, mine, other, out_rows, gain_row, skip_row, bias_row, decay_row):
    length, cp = gate.shape
    model = mine.shape[1]
    blocks = length // BLOCK
    wide = rows_spec(cp, blocks)
    half = halves_spec(seqs, blocks, model)
    return call(
        mix_kernel,
        "mix",
        15,
        blocks,
        [
            (starts, SCALARS),
            (place, SCALARS),
            (act, rows_spec(act.shape[1], blocks)),
            (gate, wide),
            (step, pl.BlockSpec((step.shape[0], BLOCK), lambda i: (0, i))),
            (mine, half),
            (other, half),
            (out_rows, None),
            (gain_row, None),
            (skip_row, None),
            (bias_row, None),
            (decay_row, None),
        ],
        [
            ((length, cp), F32, wide),
            ((length, cp), BF16, wide),
            ((length, cp), BF16, wide),
            ((length, model), BF16, rows_spec(model, blocks)),
            ((length, model), BF16, rows_spec(model, blocks)),
            ((8, length), F32, pl.BlockSpec((8, BLOCK), lambda i: (0, i))),
            ((blocks, LANES, cp), F32, pl.BlockSpec((1, LANES, cp), lambda i: (i, 0, 0))),
        ],
        [
            ((LANES, cp), F32),
            ((BLOCK, cp), F32),
            ((BLOCK, cp), F32),
            ((BLOCK, cp), BF16),
            ((BLOCK, cp), BF16),
        ],
    )


def ungate_rows(inner, stats, more, gate, mixed, dy, gain_row):
    length, cp = gate.shape
    blocks = length // BLOCK
    wide = rows_spec(cp, blocks)
    return call(
        partial(ungate_kernel, inner),
        "ungate",
        6,
        blocks,
        [(v, pl.BlockSpec((8, BLOCK), lambda i: (0, i))) for v in (stats, more)]
        + [(gate, wide), (mixed, wide), (dy, wide), (gain_row, None)],
        [((length, cp), BF16, wide)] * 3,
        [],
    )


def unmix_rows(
    seqs, per, owners, starts, place, act, step, dmix, y, states, slope, conv_in, taps, skip_row, bias_row, decay_row
):
    length, cp = dmix.shape
    cc = act.shape[1]
    blocks = length // BLOCK
    wide = rows_spec(cp, blocks, True)
    channels = rows_spec(cc, blocks, True)
    return call(
        partial(unmix_kernel, seqs, per),
        "unmix",
        28,
        blocks,
        [
            (starts, SCALARS),
            (place, SCALARS),
            (act, channels),
            (step, pl.BlockSpec((step.shape[0], BLOCK), lambda i: (0, blocks - 1 - i))),
            (dmix, wide),
            (y, wide),
            (states, pl.BlockSpec((1, LANES, cp), lambda i: (blocks - 1 - i, 0, 0))),
            (slope, channels),
            (conv_in, channels),
            (taps, None),
            (skip_row, None),
            (bias_row, None),
            (decay_row, None),
        ],
        [
            ((length, cc + LANES), BF16, rows_spec(cc + LANES, blocks, True)),
            ((owners, 8, LANES), F32, None),
        ],
        [
            ((LANES, cp), F32),
            ((BLOCK, cp), F32),
            ((BLOCK, cp), F32),
            ((BLOCK, cp), BF16),
            ((BLOCK, cp), BF16),
            ((BLOCK, cp), BF16),
            ((BLOCK, cp), F32),
            ((BLOCK, cp), F32),
            ((BLOCK, cp), F32),
            ((8, cp), F32),
            ((cc // LANES, BLOCK + 8, LANES), F32),
            ((TAPS + 1, 8, cc), F32),
            ((8, cp), F32),
            (bias_row.shape, F32),
            (bias_row.shape, F32),
        ],
    )


def back_rows(part, parts, dgate, dproj, weights):
    length, cp = dgate.shape
    model = weights.shape[0]
    tall = 2 * BLOCK if parts == 2 else BLOCK
    blocks = length // parts // tall

    def at(i, part_ref):
        return (part_ref[0] * blocks + i, 0)

    return pl.pallas_call(
        lambda part_ref, *refs: back_kernel(*refs),
        grid_spec=pltpu.PrefetchScalarGridSpec(
            num_scalar_prefetch=1,
            grid=(blocks,),
            in_specs=[
                pl.BlockSpec((tall, cp), at),
                pl.BlockSpec((tall, dproj.shape[1]), at),
                pl.BlockSpec(weights.shape, lambda i, part_ref: (0, 0)),
            ],
            out_specs=pl.BlockSpec((tall, model), lambda i, part_ref: (i, 0)),
        ),
        out_shape=jax.ShapeDtypeStruct((length // parts, model), BF16),
        cost_estimate=pl.CostEstimate(flops=4000000000, bytes_accessed=12000000, transcendentals=0),
        compiler_params=pltpu.CompilerParams(vmem_limit_bytes=VMEM_LIMIT),
        name="back",
    )(part, dgate, dproj, weights)


def swap_bit(v, bit):
    count = lax.axis_size("fsdp")
    return lax.ppermute(v, "fsdp", [(i, i ^ (1 << bit)) for i in range(count)])


def halve(v, bits, left=None):
    count = lax.axis_size("fsdp").bit_length() - 1
    place = lax.axis_index("fsdp")
    left = list(range(count)) if left is None else list(left)
    for bit in bits:
        axis = len(left) - 1 - left.index(bit)
        left.remove(bit)
        mine = (place >> bit) & 1
        kept = lax.dynamic_index_in_dim(v, mine, axis, False)
        sent = lax.dynamic_index_in_dim(v, 1 - mine, axis, False)
        v = kept + swap_bit(sent, bit)
    return v


def by_bits(v):
    bits = v.shape[0].bit_length() - 1
    return v.reshape((2,) * bits + v.shape[1:])


def tied(*values):
    return lax.optimization_barrier(values)


class Ring:
    def __init__(self, v):
        count = lax.axis_size("fsdp")
        self.chips = count // 2
        place = lax.axis_index("fsdp")
        self.chip, self.core = place // 2, place % 2
        self.walk = list(range(0, self.chips, 2)) + list(range(1, self.chips, 2))[::-1]
        self.here = jnp.where(self.chip % 2 == 0, self.chip // 2, self.chips - 1 - self.chip // 2)
        self.up = self.down = v
        self.steps = 0
        self.found = []
        self.put(0, v)

    def chip_at(self, step):
        spot = (self.here + step) % self.chips
        return jnp.where(spot < (self.chips + 1) // 2, 2 * spot, 2 * (self.chips - 1 - spot) + 1)

    def turn(self, block, way):
        pairs = [
            (self.walk[i] * 2 + c, self.walk[(i + way) % self.chips] * 2 + c)
            for i in range(self.chips)
            for c in range(2)
        ]
        return lax.ppermute(block, "fsdp", pairs)

    def put(self, step, block):
        source = self.chip_at(step) * 2
        self.found.append((source + self.core, block))
        self.found.append((source + 1 - self.core, swap_bit(block, 0)))

    def step(self):
        self.steps += 1
        if 2 * self.steps < self.chips:
            self.up = self.turn(self.up, 1)
            self.down = self.turn(self.down, -1)
            self.put(-self.steps, self.up)
            self.put(self.steps, self.down)
        elif 2 * self.steps == self.chips:
            self.put(self.steps, self.turn(self.up, 1))

    def run(self, steps):
        for _ in range(steps):
            self.step()
        return self.found


def seq_swap(v):
    return lax.ppermute(v, "seq", [(0, 1), (1, 0)])


def seq_gather(v):
    if lax.axis_size("seq") != 2:
        return lax.all_gather(v, "seq", axis=0)
    other = seq_swap(v)
    low = lax.axis_index("seq") == 0
    return jnp.stack([jnp.where(low, v, other), jnp.where(low, other, v)])


def seq_scatter(v, axis):
    count = lax.axis_size("seq")
    if count != 2:
        return lax.psum_scatter(v, "seq", scatter_dimension=axis, tiled=True).astype(F32)
    place = lax.axis_index("seq")
    size = v.shape[axis] // 2
    sent = lax.dynamic_slice_in_dim(v, (1 - place) * size, size, axis)
    kept = lax.dynamic_slice_in_dim(v, place * size, size, axis)
    return kept.astype(F32) + seq_swap(sent).astype(F32)


def widen(v, width):
    if v.shape[-1] == width:
        return v
    return jnp.pad(v, [(0, 0)] * (v.ndim - 1) + [(0, width - v.shape[-1])])


def body(
    block_in,
    grad_out,
    doc_starts,
    in_weight,
    out_weight,
    conv_weight,
    conv_bias,
    norm_gain,
    gate_gain,
    decay_log,
    skip_gain,
    step_bias,
):
    seqs = lax.axis_size("seq")
    owners = lax.axis_size("fsdp")
    place = lax.axis_index("seq")
    rows_here, model = block_in.shape[1:]
    length = rows_here * seqs
    heads = decay_log.shape[0]
    heads_here = heads // seqs
    inner = out_weight.shape[0] * owners
    channels = conv_weight.shape[1] * owners
    states = channels - inner
    cg = heads_here * HEAD
    cp = -(-cg // LANES) * LANES
    cc = cp + states
    starts = doc_starts[0]

    shard, per = in_weight.shape[0], conv_bias.shape[0]
    place_row = place.reshape(1).astype(jnp.int32)
    out_piece = lax.dynamic_index_in_dim(out_weight.reshape(seqs, cg // owners, model), place, 0, False)
    out_piece = lax.ppermute(
        out_piece,
        ("seq", "fsdp"),
        [(s * owners + h, seqs * h + s) for s in range(seqs) for h in range(owners)],
    )
    own = pack_rows(
        seqs,
        place_row,
        in_weight,
        out_piece.reshape(shard, cg),
        conv_weight,
        conv_bias[None],
        norm_gain[None],
        gate_gain[None],
        states,
    )
    ring = Ring(own)
    if seqs == 2:
        tokens, others = block_in[0], seq_swap(block_in[0])
    else:
        tokens = others = lax.all_gather(block_in[0], "seq", axis=0, tiled=True)
    ring.run(min(2, owners // 4))
    grads = grad_out[0]
    ring.up, grads = tied(ring.up, grads)
    if seqs == 2:
        other_grads = seq_swap(grads)
    else:
        grads = other_grads = lax.all_gather(grads, "seq", axis=0, tiled=True)
    found = ring.run(owners // 4 - ring.steps)
    if cg == cp and cg // owners == shard and shard % 16 == 0:
        places = jnp.stack([spot for spot, _ in found])
        normed, gate, conv_in, act, slope, step, weights, out_rows, taps, norm_row, gain_row = enter_rows(
            seqs, per, starts, place_row, places, tokens, others, [v for _, v in found], None, None, None,
            length, cp, cc, inner,
        )
    else:
        gathered = jnp.zeros((owners,) + own.shape, BF16)
        for spot, v in found:
            gathered = lax.dynamic_update_index_in_dim(gathered, v, spot, 0)
        weights = gathered[:, :, : cp + cc + LANES].reshape(model, -1)
        out_rows = gathered[:, :, cp + cc + LANES : cp + cc + LANES + cg].reshape(cg, model)
        out_rows = jnp.pad(out_rows, ((0, cp - cg), (0, 0)))
        sides = gathered[:, :8, cp + cc + LANES - per : cp + cc + LANES].astype(F32)
        taps = sides.transpose(1, 0, 2).reshape(8, channels)
        taps = jnp.concatenate(
            [widen(lax.dynamic_slice_in_dim(taps, place * cg, cg, 1), cp), taps[:, inner:]], axis=1
        )
        norm_row = sides[:, TAPS + 1, :shard].reshape(1, model)
        gain_row = sides[:, TAPS + 2, : gate_gain.shape[0]].reshape(1, inner)
        gain_row = widen(lax.dynamic_slice_in_dim(gain_row, place * cg, cg, 1), cp)
        normed, gate, conv_in, act, slope, step = enter_rows(
            seqs, per, starts, place_row, None, tokens, others, None, norm_row, weights, taps, length, cp, cc, inner
        )

    def my_heads(v):
        return lax.dynamic_slice_in_dim(v, place * heads_here, heads_here)

    skip_row = widen(jnp.repeat(my_heads(skip_gain), HEAD)[None], cp)
    many = -(-(cp // HEAD) // 8) * 8

    def by_heads(v):
        return jnp.broadcast_to(widen(my_heads(v)[None], many).reshape(many, 1), (many, BLOCK))

    decay_row, step_row = by_heads(decay_log), by_heads(step_bias)

    y, mixed, dy, grads, partial_out, stats, states_kept = mix_rows(
        seqs, starts, place_row, act, gate, step, grads, other_grads, out_rows, gain_row, skip_row, step_row, decay_row
    )
    if seqs == 2:
        more = seq_swap(stats)
    else:
        stats, more = lax.psum(stats, "seq"), jnp.zeros_like(stats)
    out_sum = seq_scatter(partial_out, 0)
    squares = lax.dynamic_slice_in_dim(stats[0] + more[0], place * rows_here, rows_here)
    out_scale = lax.rsqrt(squares / inner + EPS)
    block_out = (block_in[0].astype(F32) + out_scale[:, None] * out_sum).astype(BF16)[None]

    bits = owners.bit_length() - 1
    dgate, dmix, gate_normed = ungate_rows(inner, stats, more, gate, mixed, dy, gain_row)
    early = by_bits(
        jnp.concatenate(
            [
                dot_tn(normed, dgate).astype(BF16).reshape(owners, shard, cp),
                dot_tn(gate_normed, grads).astype(BF16)[:cg].reshape(owners, shard, cg),
            ],
            axis=2,
        )
    )
    early = halve(early, [1])
    dproj, small_grads = unmix_rows(
        seqs, per, owners, starts, place_row, act, step, dmix, y, states_kept, slope, conv_in, taps,
        skip_row, step_row, decay_row,
    )
    dproj, early, out_sum = tied(dproj, early, out_sum)
    early = halve(early, [0], [0, *range(2, bits)])
    late = dot_tn(normed, dproj).astype(BF16).reshape(owners, shard, cc + LANES)
    late = late + jnp.pad(small_grads.astype(BF16), ((0, 0), (0, shard - 8), (cc, 0)))
    late = halve(by_bits(late), [0])
    late, early = tied(late, early)
    late = halve(late, [1], range(1, bits))
    early = halve(early, [2], range(2, bits))
    if seqs == 2:
        sent = back_rows(1 - place_row, 2, dgate, dproj, weights)
        kept = back_rows(place_row, 2, dgate, dproj, weights)
        got = seq_swap(sent)
    else:
        d_normed = back_rows(jnp.zeros_like(place_row), 1, dgate, dproj, weights)
        kept, got = lax.psum_scatter(d_normed, "seq", scatter_dimension=0, tiled=True), None
    kept, late, early = tied(kept, late, early)
    late = halve(late, [2], range(2, bits))
    early = halve(early, range(3, bits), range(3, bits))
    late = halve(late, range(3, bits), range(3, bits))
    if got is not None:
        late, got = tied(late, got)
    late, early = tied(late, early)
    late_all = seq_gather(jnp.concatenate([early[:, :cp], late], axis=1)).astype(F32)
    piece = early[:, cp:].reshape(cg // owners, model)
    found = []
    for turn in range(seqs):
        pairs = []
        for q in range(seqs * owners):
            pairs.append((q, ((q + turn) % seqs) * owners + q // seqs))
        found.append(lax.ppermute(piece, ("seq", "fsdp"), pairs))
    d_normed_mine = kept.astype(F32)
    if got is not None:
        d_normed_mine = d_normed_mine + got.astype(F32)

    early_all, late_all = late_all[:, :, :cg], late_all[:, :, cp:]

    def columns(v):
        return jnp.concatenate([v[i] for i in range(seqs)], axis=1)

    in_grad = jnp.concatenate(
        [
            columns(early_all),
            columns(late_all[:, :, :cg]),
            jnp.sum(late_all[:, :, cp:cc], axis=0),
            columns(late_all[:, :, cc : cc + heads_here]),
        ],
        axis=1,
    )
    norm_grad = jnp.sum(in_grad * in_weight.astype(F32), axis=1) / norm_gain.astype(F32)
    small_sums = jnp.sum(late_all[:, :8, cc + LANES - per :], axis=0)
    head_out = small_sums[TAPS + 1 : TAPS + 4, :heads]

    found = jnp.stack(found)
    out_grad = jnp.concatenate(
        [lax.dynamic_index_in_dim(found, (place - i) % seqs, 0, False) for i in range(seqs)], axis=0
    ).astype(F32)
    gain_grad = jnp.sum(out_grad * out_weight.astype(F32), axis=1) / gate_gain.astype(F32)

    x = block_in[0].astype(F32)
    scale = lax.rsqrt(jnp.mean(x * x, axis=-1, keepdims=True) + EPS)
    gained = d_normed_mine * norm_row
    along = scale * scale * jnp.mean(gained * x, axis=-1, keepdims=True)
    grad_in = (grad_out[0].astype(F32) + scale * (gained - x * along)).astype(BF16)[None]

    return (
        block_out,
        grad_in,
        in_grad,
        out_grad,
        small_sums[:TAPS],
        small_sums[TAPS],
        norm_grad,
        gain_grad,
        head_out[0],
        head_out[2],
        head_out[1],
    )


def solution(mesh):
    placed = (
        P("fsdp", "seq", None),
        P("fsdp", "seq", None),
        P("fsdp", None),
        P("fsdp", None),
        P("fsdp", None),
        P(None, "fsdp"),
        P("fsdp"),
        P("fsdp"),
        P("fsdp"),
        P(),
        P(),
        P(),
    )
    return jax.shard_map(
        body,
        mesh=mesh,
        in_specs=placed,
        out_specs=(
            P("fsdp", "seq", None),
            P("fsdp", "seq", None),
            P("fsdp", None),
            P("fsdp", None),
            P(None, "fsdp"),
            P("fsdp"),
            P("fsdp"),
            P("fsdp"),
            P(),
            P(),
            P(),
        ),
        check_vma=False,
    )
```

```python
from functools import partial

import jax
import jax.numpy as jnp
from jax import lax
from jax.experimental import pallas as pl
from jax.experimental.pallas import tpu as pltpu
from jax.sharding import PartitionSpec as P

BLOCK = 256
LANES = 128
HEAD = 64
TAPS = 4
EPS = 1e-05
FAR = -1e30
LOG2E = 1.4426950408889634
VMEM_LIMIT = 22 * 1024 * 1024
F32 = jnp.float32
BF16 = jnp.bfloat16


def dot(a, b):
    return jnp.dot(a, b, preferred_element_type=F32)


def dot_nt(a, b):
    return lax.dot_general(a, b, (((1,), (1,)), ((), ())), preferred_element_type=F32)


def dot_tn(a, b):
    return lax.dot_general(a, b, (((0,), (0,)), ((), ())), preferred_element_type=F32)


def split_dot(product, left, values, parts):
    total = None
    rest = values
    for _ in range(parts):
        term = rest.astype(BF16)
        rest = rest - term.astype(F32)
        piece = product(left, term)
        total = piece if total is None else total + piece
    return total


def sigmoid(v):
    return 0.5 + 0.5 * jnp.tanh(0.5 * v)


def softplus(v):
    t = jnp.exp(-jnp.abs(v))
    small = t * (1.0 - t * (0.5 - t * (1.0 / 3.0 - t * 0.25)))
    return jnp.maximum(v, 0.0) + jnp.where(t < 0.01, small, jnp.log(1.0 + t))


def doc_count(starts, place):
    total = (place >= starts[0]).astype(jnp.int32)
    for k in range(1, starts.shape[0]):
        total = total + (place >= starts[k]).astype(jnp.int32)
    return total


def doc_masks(starts, place, ahead):
    edge = jnp.full(place.shape, 2**30 if ahead else 0, jnp.int32)
    for k in range(starts.shape[0]):
        if ahead:
            edge = jnp.minimum(edge, jnp.where(starts[k] > place, starts[k], 2**30))
        else:
            edge = jnp.maximum(edge, jnp.where(starts[k] <= place, starts[k], 0))
    room = edge - place - 1 if ahead else place - edge
    return [jnp.where(room >= back, 1.0, 0.0) for back in range(1, TAPS)]


def head_pair(values, pair, left):
    return jnp.where(left, values[:, 2 * pair : 2 * pair + 1], values[:, 2 * pair + 1 : 2 * pair + 2])


def head_column(values, head):
    return jnp.broadcast_to(values[:, head : head + 1], (values.shape[0], LANES))


def lane_left(rows):
    return lax.broadcasted_iota(jnp.int32, (rows, LANES), 1) < HEAD


def pack_kernel(
    seqs, place_ref, in_ref, out_ref, taps_ref, bias_ref, norm_ref, gain_ref, own_ref, tile
):
    cg, per = out_ref.shape[1], taps_ref.shape[1]
    cp = -(-cg // LANES) * LANES
    inner = cg * seqs
    heads = cg // HEAD
    states = own_ref.shape[1] - 3 * cp - LANES
    if cp != cg:
        own_ref[...] = jnp.zeros_like(own_ref)
    tile[...] = jnp.zeros_like(tile)
    at = 2 * inner + states
    for s in range(seqs):

        @pl.when(place_ref[0] == s)
        def _():
            own_ref[:, :cg] = in_ref[:, s * cg : (s + 1) * cg]
            own_ref[:, cp : cp + cg] = in_ref[:, inner + s * cg : inner + (s + 1) * cg]
            tile[:, :heads] = in_ref[:, at + s * heads : at + (s + 1) * heads].astype(F32)

    own_ref[:, 2 * cp : 2 * cp + states] = in_ref[:, 2 * inner : at]
    tile[:TAPS, LANES - per :] = taps_ref[...].astype(F32)
    tile[TAPS : TAPS + 1, LANES - per :] = bias_ref[...].astype(F32)
    tile[TAPS + 1 : TAPS + 2, LANES - per : LANES - per + norm_ref.shape[1]] = norm_ref[...].astype(F32)
    tile[TAPS + 2 : TAPS + 3, LANES - per : LANES - per + gain_ref.shape[1]] = gain_ref[...].astype(F32)
    own_ref[:, 2 * cp + states : 2 * cp + states + LANES] = tile[...].astype(BF16)
    own_ref[:, 2 * cp + states + LANES : 2 * cp + states + LANES + cg] = out_ref[...]


def assemble(
    seqs, per, places, place_ref, blocks, w_ref, wo_ref, taps_ref, norm_ref, gain_ref, taps_all, gain_all, sems
):
    count = len(blocks)
    shard = blocks[0].shape[0]
    width = w_ref.shape[1]
    copies = []
    for k, block in enumerate(blocks):
        rows = pl.ds(pl.multiple_of(places[k] * shard, 16), shard)
        copies.append(pltpu.make_async_copy(block.at[:, :width], w_ref.at[rows, :], sems.at[2 * k]))
        copies.append(pltpu.make_async_copy(block.at[:, width:], wo_ref.at[rows, :], sems.at[2 * k + 1]))
    for copy in copies:
        copy.start()
    for copy in copies:
        copy.wait()
    some = gain_all.shape[1] // count
    for f in range(count):
        side = w_ref[f * shard : f * shard + 16, width - LANES :].astype(F32)[:, LANES - per :]
        taps_all[:8, f * per : (f + 1) * per] = side[:8, :]
        norm_ref[:, f * shard : (f + 1) * shard] = side[TAPS + 1 : TAPS + 2, :shard]
        gain_all[:, f * some : (f + 1) * some] = side[TAPS + 2 : TAPS + 3, :some]
    cp = gain_ref.shape[1]
    taps_ref[:, cp:] = taps_all[:, cp * seqs :]
    for s in range(seqs):

        @pl.when(place_ref[0] == s)
        def _():
            taps_ref[:, :cp] = taps_all[:, s * cp : (s + 1) * cp]
            gain_ref[...] = gain_all[:, s * cp : (s + 1) * cp]


def first_entry_kernel(seqs, per, count, starts, places, place_ref, mine_ref, other_ref, *refs):
    blocks = refs[:count]
    outs, (w_out, wo_out, taps_ref, norm_ref, gain_ref) = refs[count : count + 6], refs[count + 6 : count + 11]
    buf, w_ref, wo_ref, taps_all, gain_all, sems, sems_in = refs[count + 11 :]
    copies = [
        pltpu.make_async_copy(w_ref, w_out, sems.at[0]),
        pltpu.make_async_copy(wo_ref, wo_out, sems.at[1]),
    ]

    @pl.when(pl.program_id(0) == 0)
    def _():
        assemble(
            seqs, per, places, place_ref, blocks, w_ref, wo_ref, taps_ref, norm_ref, gain_ref, taps_all, gain_all, sems_in
        )
        for copy in copies:
            copy.start()

    entry_kernel(starts, place_ref, mine_ref, other_ref, norm_ref, w_ref, taps_ref, *outs, buf)

    @pl.when(pl.program_id(0) == pl.num_programs(0) - 1)
    def _():
        for copy in copies:
            copy.wait()


def row_block(place_ref, block, mine_ref, other_ref):
    mine = 2 * block // pl.num_programs(0) == place_ref[0]
    return jnp.where(mine, mine_ref[...].astype(F32), other_ref[...].astype(F32))


def entry_kernel(
    starts, place_ref, mine_ref, other_ref, norm_ref, w_ref, taps_ref,
    xn_ref, gate_ref, ci_ref, act_ref, slope_ref, step_ref, buf,
):
    block = pl.program_id(0)
    cp = gate_ref.shape[1]
    cc = act_ref.shape[1]
    x = row_block(place_ref, block, mine_ref, other_ref)
    scale = lax.rsqrt(jnp.mean(x * x, axis=-1, keepdims=True) + EPS)
    xn = (x * scale * norm_ref[...]).astype(BF16)
    xn_ref[...] = xn
    gate_ref[...] = dot(xn, w_ref[:, :cp]).astype(BF16)
    step = dot(xn, w_ref[:, cp + cc :]).astype(BF16).astype(F32)
    step_ref[...] = jnp.transpose(step)[: step_ref.shape[0], :]

    @pl.when(block == 0)
    def _():
        buf[:, :8, :] = jnp.zeros((cc // LANES, 8, LANES), F32)

    @pl.when(block > 0)
    def _():
        buf[:, :8, :] = buf[:, BLOCK : BLOCK + 8, :]

    ci = dot(xn, w_ref[:, cp : cp + cc]).astype(BF16)
    ci_ref[...] = ci
    place = block * BLOCK + lax.broadcasted_iota(jnp.int32, (BLOCK, LANES), 0)
    masks = doc_masks(starts, place, False)
    for tile in range(cc // LANES):
        cols = slice(tile * LANES, (tile + 1) * LANES)
        here = ci[:, cols].astype(F32)
        buf[tile, 8:, :] = here
        total = taps_ref[TAPS : TAPS + 1, cols] + taps_ref[TAPS - 1 : TAPS, cols] * here
        for back in range(1, TAPS):
            tap = taps_ref[TAPS - 1 - back : TAPS - back, cols]
            total = total + masks[back - 1] * tap * buf[tile, 8 - back : 8 - back + BLOCK, :]
        sig = sigmoid(total)
        act_ref[:, cols] = (total * sig).astype(BF16)
        slope_ref[:, cols] = (sig * (1.0 + total * (1.0 - sig))).astype(BF16)


def tri(upper):
    rows = lax.broadcasted_iota(jnp.int32, (BLOCK, BLOCK), 0)
    cols = lax.broadcasted_iota(jnp.int32, (BLOCK, BLOCK), 1)
    return rows <= cols if upper else rows >= cols


def as_columns(*rows):
    stack = jnp.concatenate(rows, axis=0)
    rest = LANES - stack.shape[0]
    return jnp.transpose(jnp.concatenate([stack, jnp.zeros((rest, BLOCK), F32)], axis=0))


def block_decays(starts, block, step_ref, bias_ref, decay_ref):
    raw = step_ref[...] + bias_ref[...]
    step = softplus(raw)
    rate = -jnp.exp(decay_ref[...])
    log_decay = rate * step
    ones = jnp.where(tri(True), 1.0, 0.0).astype(BF16)
    running = split_dot(lambda m, v: dot(v, m), ones, log_decay * LOG2E, 3)
    return raw, step, rate, log_decay, running


def block_docs(starts, block, upper):
    base = block * BLOCK
    place = base + lax.broadcasted_iota(jnp.int32, (BLOCK, LANES), 0)
    docs = doc_count(starts, place)
    docs_row = doc_count(starts, base + lax.broadcasted_iota(jnp.int32, (1, BLOCK), 1))
    prev = doc_count(starts, base - 1)
    last = doc_count(starts, base + BLOCK - 1)
    docs_wide = jnp.concatenate([docs] * (BLOCK // LANES), axis=1)
    penalty = jnp.where(tri(upper) & (docs_wide == docs_row), 0.0, FAR)
    enter = jnp.where(docs == prev, 0.0, FAR)
    leave = jnp.where(docs == last, 0.0, FAR)
    return place, penalty, enter, leave, jnp.where(last == prev, 1.0, 0.0)


def halves(upper):
    half = BLOCK // 2
    if upper:
        return [(slice(0, half), slice(0, BLOCK)), (slice(half, BLOCK), slice(half, BLOCK))]
    return [(slice(0, half), slice(0, half)), (slice(half, BLOCK), slice(0, BLOCK))]


def wide_column(column, down, along):
    return jnp.concatenate([column[down, :]] * ((along.stop - along.start) // LANES), axis=1)


def mix_kernel(
    starts, place_ref, act_ref, gate_ref, step_ref, mine_ref, other_ref, wout_ref, gain_ref, skip_ref, bias_ref,
    decay_ref,
    y_ref, mixed_ref, dy_ref, g_ref, u_ref, stats_ref, state_ref, carry, from_state, dy_full, xw_full, gated_full,
):
    block = pl.program_id(0)
    cp = gate_ref.shape[1]
    raw, step, rate, log_decay, running = block_decays(starts, block, step_ref, bias_ref, decay_ref)
    place, penalty, enter, leave, through = block_docs(starts, block, False)
    many = step.shape[0]
    columns = as_columns(running, step)
    final = columns[BLOCK - 1 : BLOCK, :]

    @pl.when(block == 0)
    def _():
        carry[...] = jnp.zeros_like(carry)

    state_ref[0] = carry[...]
    state_in = act_ref[:, cp : cp + LANES]
    state_out = act_ref[:, cp + LANES : cp + 2 * LANES]
    scores = dot_nt(state_out, state_in)
    from_state[...] = dot(state_out, carry[...].astype(BF16))
    grad = row_block(place_ref, block, mine_ref, other_ref).astype(BF16)
    g_ref[...] = grad
    dy_full[...] = dot_nt(grad, wout_ref[...])
    left = lane_left(BLOCK)
    left_row = lane_left(1)
    squares = jnp.zeros((BLOCK, LANES), F32)
    crosses = jnp.zeros((BLOCK, LANES), F32)
    for pair in range(cp // LANES):
        lanes = slice(pair * LANES, (pair + 1) * LANES)
        x = act_ref[:, lanes].astype(F32)
        xs = (x * jnp.where(left, head_column(columns, many + 2 * pair), head_column(columns, many + 2 * pair + 1))).astype(BF16)
        sums = [head_column(columns, 2 * pair), head_column(columns, 2 * pair + 1)]
        both = jnp.where(left, sums[0], sums[1])
        within = None
        for side in range(2):
            head = 2 * pair + side
            strips = []
            for down, along in halves(False):
                gaps = wide_column(sums[side], down, along) - running[head : head + 1, along] + penalty[down, along]
                mix = (scores[down, along] * jnp.exp2(gaps)).astype(BF16)
                strips.append(dot(mix, xs[along, :]))
            part = jnp.concatenate(strips, axis=0)
            within = part if side == 0 else jnp.where(left, within, part)
        y = within + jnp.exp2(both + enter) * from_state[:, lanes]
        y_ref[:, lanes] = y
        xw_full[:, lanes] = (xs.astype(F32) * jnp.exp2(head_pair(final, pair, left_row) - both + leave)).astype(BF16)
        mixed = (y + skip_ref[:, lanes] * x).astype(BF16)
        mixed_ref[:, lanes] = mixed
        gate = gate_ref[:, lanes].astype(F32)
        gated = mixed.astype(F32) * gate * sigmoid(gate)
        dy = dy_full[:, lanes]
        dy_ref[:, lanes] = dy.astype(BF16)
        gained = gated * gain_ref[:, lanes]
        squares = squares + gated * gated
        crosses = crosses + dy * gained
        gated_full[:, lanes] = gained.astype(BF16)
    state_in_t = jnp.transpose(state_in.astype(F32)).astype(BF16)
    added = dot(state_in_t, xw_full[...])
    for pair in range(cp // LANES):
        lanes = slice(pair * LANES, (pair + 1) * LANES)
        kept = through * jnp.exp2(head_pair(final, pair, left_row))
        carry[:, lanes] = kept * carry[:, lanes] + added[:, lanes]
    u_ref[...] = dot(gated_full[...], wout_ref[...]).astype(BF16)
    lane = lax.broadcasted_iota(jnp.int32, (BLOCK, LANES), 1)
    sums = jnp.where(lane == 0, jnp.sum(squares, axis=1, keepdims=True), 0.0) + jnp.where(
        lane == 1, jnp.sum(crosses, axis=1, keepdims=True), 0.0
    )
    stats_ref[...] = jnp.transpose(sums)[:8, :]


def ungate_kernel(inner, stats_ref, more_ref, gate_ref, mixed_ref, dy_ref, gain_ref, dgate_ref, dmix_ref, gn_ref):
    cp = gate_ref.shape[1]
    stats = stats_ref[...] + more_ref[...]
    stats = jnp.transpose(jnp.concatenate([stats, jnp.zeros((LANES - 8, BLOCK), F32)], axis=0))
    scale = lax.rsqrt(stats[:, 0:1] / inner + EPS)
    pull = scale * scale * scale * stats[:, 1:2] / inner
    for pair in range(cp // LANES):
        lanes = slice(pair * LANES, (pair + 1) * LANES)
        gate = gate_ref[:, lanes].astype(F32)
        mixed = mixed_ref[:, lanes].astype(F32)
        sig = sigmoid(gate)
        silu = gate * sig
        gated = mixed * silu
        gain = gain_ref[:, lanes]
        gn_ref[:, lanes] = (gated * scale * gain).astype(BF16)
        d_gated = scale * gain * dy_ref[:, lanes].astype(F32) - gated * pull
        dmix_ref[:, lanes] = (d_gated * silu).astype(BF16)
        dgate_ref[:, lanes] = (d_gated * mixed * (sig * (1.0 + gate * (1.0 - sig)))).astype(BF16)


def tall_sum(v):
    return jnp.sum(v.reshape(v.shape[0] // 8, 8, v.shape[1]), axis=0)


def conv_back(d_conv, ci, masks, taps_ref, buf, sums, tile):
    lanes = slice(tile * LANES, (tile + 1) * LANES)
    sums[TAPS - 1, :, lanes] += tall_sum(d_conv * ci)
    sums[TAPS, :, lanes] += tall_sum(d_conv)
    total = d_conv * taps_ref[TAPS - 1 : TAPS, lanes]
    buf[tile, :BLOCK, :] = d_conv
    for back in range(1, TAPS):
        tap = TAPS - 1 - back
        later = buf[tile, back : back + BLOCK, :] * masks[back - 1]
        sums[tap, :, lanes] += tall_sum(later * ci)
        total = total + taps_ref[tap : tap + 1, lanes] * later
    return total.astype(BF16)


def carry_rims(turn, buf):
    @pl.when(turn == 0)
    def _():
        buf[:, BLOCK:, :] = jnp.zeros((buf.shape[0], 8, LANES), F32)

    @pl.when(turn > 0)
    def _():
        buf[:, BLOCK:, :] = buf[:, :8, :]


def unmix_kernel(
    seqs, per, starts, place_ref, act_ref, step_ref, dmix_ref, y_ref, state_ref, slope_ref, ci_ref, taps_ref,
    skip_ref, bias_ref, decay_ref,
    dproj_ref, small_ref,
    carry, first, second, enter_full, xs_full, xw_full, spread_full, step_full, leave_full, wide, buf, sums,
    skips, decays, biases,
):
    turn = pl.program_id(0)
    turns = pl.num_programs(0)
    block = turns - 1 - turn
    cp = dmix_ref.shape[1]
    raw, step, rate, log_decay, running = block_decays(starts, block, step_ref, bias_ref, decay_ref)
    place, penalty, enter, leave, through = block_docs(starts, block, True)
    many = step.shape[0]
    columns = as_columns(running, step)
    final = columns[BLOCK - 1 : BLOCK, :]

    @pl.when(turn == 0)
    def _():
        carry[...] = jnp.zeros_like(carry)
        sums[...] = jnp.zeros_like(sums)
        skips[...] = jnp.zeros_like(skips)
        decays[...] = jnp.zeros_like(decays)
        biases[...] = jnp.zeros_like(biases)

    carry_rims(turn, buf)
    state_in = act_ref[:, cp : cp + LANES]
    state_out = act_ref[:, cp + LANES : cp + 2 * LANES]
    scores_t = dot_nt(state_in, state_out)
    masks = doc_masks(starts, place, True)
    state_out_t = jnp.transpose(state_out.astype(F32)).astype(BF16)
    left = lane_left(BLOCK)
    left_row = lane_left(1)
    for pair in range(cp // LANES):
        lanes = slice(pair * LANES, (pair + 1) * LANES)
        step_b = jnp.where(left, head_column(columns, many + 2 * pair), head_column(columns, many + 2 * pair + 1))
        both = jnp.where(left, head_column(columns, 2 * pair), head_column(columns, 2 * pair + 1))
        leave_b = jnp.exp2(head_pair(final, pair, left_row) - both + leave)
        step_full[:, lanes] = step_b
        leave_full[:, lanes] = leave_b
        xs = (act_ref[:, lanes].astype(F32) * step_b).astype(BF16)
        xs_full[:, lanes] = xs
        xw_full[:, lanes] = (xs.astype(F32) * leave_b).astype(BF16)
        enter_full[:, lanes] = (dmix_ref[:, lanes].astype(F32) * jnp.exp2(both + enter)).astype(BF16)
    grad_b = carry[...].astype(BF16)
    d_out = dot_nt(enter_full[...], state_ref[0].astype(BF16))
    d_in = dot_nt(xw_full[...], grad_b)
    spread_full[...] = dot(state_in, grad_b)
    added = dot(state_out_t, enter_full[...])
    d_scores = [jnp.zeros((BLOCK // 2, BLOCK), F32), jnp.zeros((BLOCK // 2, BLOCK // 2), F32)]
    for pair in range(cp // LANES):
        lanes = slice(pair * LANES, (pair + 1) * LANES)
        x = act_ref[:, lanes].astype(F32)
        dmix = dmix_ref[:, lanes]
        dmix_f = dmix.astype(F32)
        xs_f = xs_full[:, lanes].astype(F32)
        spread = leave_full[:, lanes] * spread_full[:, lanes]
        pulled = None
        for side in range(2):
            head = 2 * pair + side
            mine = left if side == 0 else ~left
            xs_side = jnp.where(mine, xs_f, 0.0).astype(BF16)
            strips = []
            column = head_column(columns, head)
            for index, (down, along) in enumerate(halves(True)):
                gaps = running[head : head + 1, along] - wide_column(column, down, along) + penalty[down, along]
                decay = jnp.exp2(gaps)
                mix = (scores_t[down, along] * decay).astype(BF16)
                strips.append(dot(mix, dmix[along, :]))
                d_scores[index] = d_scores[index] + dot_nt(xs_side[down, :], dmix[along, :]) * decay
            part = jnp.concatenate(strips, axis=0)
            pulled = part if side == 0 else jnp.where(left, pulled, part)
        pulled = pulled + spread
        dx = (step_full[:, lanes] * pulled + skip_ref[:, lanes] * dmix_f).astype(BF16)
        first[:, lanes] = dmix_f * y_ref[:, lanes] - xs_f * pulled
        second[:, lanes] = x * pulled
        grad = carry[:, lanes]
        through_b = through * jnp.exp2(head_pair(final, pair, left_row))
        wide[:, lanes] = tall_sum(xs_f * spread) + through_b * tall_sum(state_ref[0, :, lanes] * grad)
        skips[:, lanes] += tall_sum(dmix_f * x)
        carry[:, lanes] = through_b * grad + added[:, lanes]
        d_conv = dx.astype(F32) * slope_ref[:, lanes].astype(F32)
        dproj_ref[:, lanes] = conv_back(d_conv, ci_ref[:, lanes].astype(F32), masks, taps_ref, buf, sums, pair)

    half = BLOCK // 2
    d_scores_t = jnp.concatenate(
        [d_scores[0], jnp.concatenate([jnp.zeros((half, half), F32), d_scores[1]], axis=1)], axis=0
    )
    d_in = d_in + dot(d_scores_t.astype(BF16), state_out)
    d_out = d_out + dot(jnp.transpose(d_scores_t).astype(BF16), state_in)
    for part, at in ((d_in, cp), (d_out, cp + LANES)):
        lanes = slice(at, at + LANES)
        d_conv = part.astype(BF16).astype(F32) * slope_ref[:, lanes].astype(F32)
        dproj_ref[:, lanes] = conv_back(
            d_conv, ci_ref[:, lanes].astype(F32), masks, taps_ref, buf, sums, at // LANES
        )

    head_of = lax.broadcasted_iota(jnp.int32, (many, cp), 1) // HEAD
    pick = jnp.where(head_of == lax.broadcasted_iota(jnp.int32, (many, cp), 0), 1.0, 0.0).astype(BF16)
    d_cum = split_dot(dot_nt, pick, first[...], 2)
    d_step = split_dot(dot_nt, pick, second[...], 2)
    d_final = jnp.sum(split_dot(dot_nt, pick, wide[...], 3), axis=1, keepdims=True)
    ones = jnp.where(tri(False), 1.0, 0.0).astype(BF16)
    d_log = split_dot(lambda m, v: dot(v, m), ones, d_cum, 3) + d_final
    d_raw = (d_step + d_log * rate) * sigmoid(raw)
    dproj_ref[:, cp + 2 * LANES :] = as_columns(d_raw).astype(BF16)
    decays[...] += d_log * log_decay
    biases[...] += d_raw

    @pl.when(turn == turns - 1)
    def _():
        owners = small_ref.shape[0]
        edge = LANES - per
        inner = per * owners - 2 * LANES
        cg = inner // seqs
        heads = cg // HEAD
        small_ref[...] = jnp.zeros_like(small_ref)
        skip_sums = split_dot(lambda m, v: dot_nt(v, m), pick, skips[...], 3)
        head_rows = [
            jnp.sum(as_columns(decays[...]), axis=0, keepdims=True),
            jnp.sum(as_columns(biases[...]), axis=0, keepdims=True),
            jnp.sum(skip_sums, axis=0, keepdims=True),
        ]
        grads = jnp.concatenate([jnp.sum(sums[k], axis=0, keepdims=True) for k in range(TAPS + 1)], axis=0)
        for s in range(seqs):

            @pl.when(place_ref[0] == s)
            def _():
                for f in range(owners):
                    for low, high, base in ((s * cg, (s + 1) * cg, 0), (inner, per * owners, cp)):
                        a, b = max(low, f * per), min(high, (f + 1) * per)
                        if a < b:
                            small_ref[f, : TAPS + 1, edge + a - f * per : edge + b - f * per] = grads[
                                :, base + a - low : base + b - low
                            ]
                    for k, row in enumerate(head_rows):
                        small_ref[f, TAPS + 1 + k : TAPS + 2 + k, edge + s * heads : edge + (s + 1) * heads] = row[
                            :, :heads
                        ]


def back_kernel(dgate_ref, dproj_ref, w_ref, dn_ref):
    cp = dgate_ref.shape[1]
    dn_ref[...] = (dot_nt(dgate_ref[...], w_ref[:, :cp]) + dot_nt(dproj_ref[...], w_ref[:, cp:])).astype(BF16)


def call(kernel, name, micros, grid, ins, outs, scratch):
    def fixed(shape):
        return pl.BlockSpec(shape, lambda i: (0,) * len(shape))

    return pl.pallas_call(
        kernel,
        grid=(grid,),
        in_specs=[fixed(array.shape) if spec is None else spec for array, spec in ins],
        out_specs=[fixed(shape) if spec is None else spec for shape, _, spec in outs],
        out_shape=[jax.ShapeDtypeStruct(shape, kind) for shape, kind, _ in outs],
        scratch_shapes=[pltpu.VMEM(*kind) if isinstance(kind, tuple) else kind for kind in scratch],
        cost_estimate=pl.CostEstimate(
            flops=micros * 1000000000, bytes_accessed=micros * 3000000, transcendentals=0
        ),
        compiler_params=pltpu.CompilerParams(vmem_limit_bytes=VMEM_LIMIT),
        name=name,
    )(*[array for array, _ in ins])


SCALARS = pl.BlockSpec(memory_space=pltpu.SMEM)


def rows_spec(width, blocks, back=False):
    if back:
        return pl.BlockSpec((BLOCK, width), lambda i: (blocks - 1 - i, 0))
    return pl.BlockSpec((BLOCK, width), lambda i: (i, 0))


def pack_rows(seqs, place, in_weight, out_piece, taps, bias, norm, gain, states):
    shard, cg = out_piece.shape
    cp = -(-cg // LANES) * LANES
    return call(
        partial(pack_kernel, seqs),
        "pack",
        1,
        1,
        [(place, SCALARS)] + [(v, None) for v in (in_weight, out_piece, taps, bias, norm, gain)],
        [((shard, 3 * cp + states + LANES), BF16, None)],
        [((shard, LANES), F32)],
    )[0]


def halves_spec(seqs, blocks, width):
    if seqs == 2:
        return pl.BlockSpec((BLOCK, width), lambda i: (i % (blocks // 2), 0))
    return rows_spec(width, blocks)


def enter_rows(seqs, per, starts, place, places, mine, other, blocks, norm_row, weights, taps, length, cp, cc, inner):
    model = mine.shape[1]
    grid = length // BLOCK
    widths = [model, cp, cc, cc, cc]
    many = -(-(cp // HEAD) // 8) * 8
    half = halves_spec(seqs, grid, model)
    outs = [((length, width), BF16, rows_spec(width, grid)) for width in widths]
    outs.append(((many, length), F32, pl.BlockSpec((many, BLOCK), lambda i: (0, i))))
    buf = ((cc // LANES, BLOCK + 8, LANES), F32)
    if not blocks:
        ins = [(starts, SCALARS), (place, SCALARS), (mine, half), (other, half)]
        ins = ins + [(norm_row, None), (weights, None), (taps, None)]
        return call(entry_kernel, "entry", 12, grid, ins, outs, [buf])
    count = len(blocks)
    anywhere = pl.BlockSpec(memory_space=pl.ANY)
    ins = [(starts, SCALARS), (places, SCALARS), (place, SCALARS), (mine, half), (other, half)]
    width = cp + cc + LANES
    return call(
        partial(first_entry_kernel, seqs, per, count),
        "entry",
        14,
        grid,
        ins + [(v, anywhere) for v in blocks],
        outs
        + [
            ((model, width), BF16, anywhere),
            ((model, cp), BF16, anywhere),
            ((8, cc), F32, None),
            ((1, model), F32, None),
            ((1, cp), F32, None),
        ],
        [
            buf,
            ((model, width), BF16),
            ((model, cp), BF16),
            ((8, per * count), F32),
            ((1, inner), F32),
            pltpu.SemaphoreType.DMA((2,)),
            pltpu.SemaphoreType.DMA((2 * count,)),
        ],
    )


def mix_rows(seqs, starts, place, act, gate, step, mine, other, out_rows, gain_row, skip_row, bias_row, decay_row):
    length, cp = gate.shape
    model = mine.shape[1]
    blocks = length // BLOCK
    wide = rows_spec(cp, blocks)
    half = halves_spec(seqs, blocks, model)
    return call(
        mix_kernel,
        "mix",
        15,
        blocks,
        [
            (starts, SCALARS),
            (place, SCALARS),
            (act, rows_spec(act.shape[1], blocks)),
            (gate, wide),
            (step, pl.BlockSpec((step.shape[0], BLOCK), lambda i: (0, i))),
            (mine, half),
            (other, half),
            (out_rows, None),
            (gain_row, None),
            (skip_row, None),
            (bias_row, None),
            (decay_row, None),
        ],
        [
            ((length, cp), F32, wide),
            ((length, cp), BF16, wide),
            ((length, cp), BF16, wide),
            ((length, model), BF16, rows_spec(model, blocks)),
            ((length, model), BF16, rows_spec(model, blocks)),
            ((8, length), F32, pl.BlockSpec((8, BLOCK), lambda i: (0, i))),
            ((blocks, LANES, cp), F32, pl.BlockSpec((1, LANES, cp), lambda i: (i, 0, 0))),
        ],
        [
            ((LANES, cp), F32),
            ((BLOCK, cp), F32),
            ((BLOCK, cp), F32),
            ((BLOCK, cp), BF16),
            ((BLOCK, cp), BF16),
        ],
    )


def ungate_rows(inner, stats, more, gate, mixed, dy, gain_row):
    length, cp = gate.shape
    blocks = length // BLOCK
    wide = rows_spec(cp, blocks)
    return call(
        partial(ungate_kernel, inner),
        "ungate",
        6,
        blocks,
        [(v, pl.BlockSpec((8, BLOCK), lambda i: (0, i))) for v in (stats, more)]
        + [(gate, wide), (mixed, wide), (dy, wide), (gain_row, None)],
        [((length, cp), BF16, wide)] * 3,
        [],
    )


def unmix_rows(
    seqs, per, owners, starts, place, act, step, dmix, y, states, slope, conv_in, taps, skip_row, bias_row, decay_row
):
    length, cp = dmix.shape
    cc = act.shape[1]
    blocks = length // BLOCK
    wide = rows_spec(cp, blocks, True)
    channels = rows_spec(cc, blocks, True)
    return call(
        partial(unmix_kernel, seqs, per),
        "unmix",
        28,
        blocks,
        [
            (starts, SCALARS),
            (place, SCALARS),
            (act, channels),
            (step, pl.BlockSpec((step.shape[0], BLOCK), lambda i: (0, blocks - 1 - i))),
            (dmix, wide),
            (y, wide),
            (states, pl.BlockSpec((1, LANES, cp), lambda i: (blocks - 1 - i, 0, 0))),
            (slope, channels),
            (conv_in, channels),
            (taps, None),
            (skip_row, None),
            (bias_row, None),
            (decay_row, None),
        ],
        [
            ((length, cc + LANES), BF16, rows_spec(cc + LANES, blocks, True)),
            ((owners, 8, LANES), F32, None),
        ],
        [
            ((LANES, cp), F32),
            ((BLOCK, cp), F32),
            ((BLOCK, cp), F32),
            ((BLOCK, cp), BF16),
            ((BLOCK, cp), BF16),
            ((BLOCK, cp), BF16),
            ((BLOCK, cp), F32),
            ((BLOCK, cp), F32),
            ((BLOCK, cp), F32),
            ((8, cp), F32),
            ((cc // LANES, BLOCK + 8, LANES), F32),
            ((TAPS + 1, 8, cc), F32),
            ((8, cp), F32),
            (bias_row.shape, F32),
            (bias_row.shape, F32),
        ],
    )


def back_rows(part, parts, dgate, dproj, weights):
    length, cp = dgate.shape
    model = weights.shape[0]
    tall = 2 * BLOCK if parts == 2 else BLOCK
    blocks = length // parts // tall

    def at(i, part_ref):
        return (part_ref[0] * blocks + i, 0)

    return pl.pallas_call(
        lambda part_ref, *refs: back_kernel(*refs),
        grid_spec=pltpu.PrefetchScalarGridSpec(
            num_scalar_prefetch=1,
            grid=(blocks,),
            in_specs=[
                pl.BlockSpec((tall, cp), at),
                pl.BlockSpec((tall, dproj.shape[1]), at),
                pl.BlockSpec(weights.shape, lambda i, part_ref: (0, 0)),
            ],
            out_specs=pl.BlockSpec((tall, model), lambda i, part_ref: (i, 0)),
        ),
        out_shape=jax.ShapeDtypeStruct((length // parts, model), BF16),
        cost_estimate=pl.CostEstimate(flops=4000000000, bytes_accessed=12000000, transcendentals=0),
        compiler_params=pltpu.CompilerParams(vmem_limit_bytes=VMEM_LIMIT),
        name="back",
    )(part, dgate, dproj, weights)


def finish_kernel(seqs, per, heads, cg, cp, place_ref, *refs):
    shares = refs[:seqs]
    weight_ref, gain_ref, in_ref, norm_ref, taps_ref, bias_ref, *head_refs, tile = refs[seqs:]
    inner = cg * seqs
    width = shares[0].shape[1]
    cc = width - cp - LANES
    states = cc - cp
    total = shares[0][...].astype(F32)
    total = total[:, 2 * cp :]
    for share in shares[1:]:
        total = total + share[:, 2 * cp :].astype(F32)
    in_ref[:, 2 * inner : 2 * inner + states] = total[:, :states]
    tile[...] = total[:, states:]
    side = tile[:8, LANES - per :]
    taps_ref[...] = side[:TAPS, :]
    bias_ref[...] = side[TAPS : TAPS + 1, :]
    for k, ref in enumerate(head_refs):
        ref[...] = side[TAPS + 1 + k : TAPS + 2 + k, :heads]
    few = cg // HEAD
    at = 2 * inner + states
    for order in range(2 if seqs == 2 else 1):

        @pl.when((place_ref[0] == order) if seqs == 2 else (place_ref[0] >= 0))
        def _():
            for k, share in enumerate(shares):
                s = (k + order) % seqs
                in_ref[:, s * cg : (s + 1) * cg] = share[:, :cg].astype(F32)
                in_ref[:, inner + s * cg : inner + (s + 1) * cg] = share[:, cp : cp + cg].astype(F32)
                in_ref[:, at + s * few : at + (s + 1) * few] = share[:, width - LANES :].astype(F32)[:, :few]

    parts = in_ref[...] * weight_ref[...].astype(F32)
    norm_ref[...] = jnp.transpose(
        jnp.broadcast_to(jnp.sum(parts, axis=1, keepdims=True), (parts.shape[0], LANES))
    )[:1, :] / gain_ref[...].astype(F32)


def finish_rows(seqs, per, place, shares, weight, gain, heads, cg, cp, cc):
    shard = weight.shape[0]
    return call(
        partial(finish_kernel, seqs, per, heads, cg, cp),
        "finish",
        2,
        1,
        [(place, SCALARS)] + [(v, None) for v in (*shares, weight, gain[None])],
        [
            (weight.shape, F32, None),
            ((1, shard), F32, None),
            ((TAPS, per), F32, None),
            ((1, per), F32, None),
            *[((1, heads), F32, None)] * 3,
        ],
        [((shard, LANES), F32)],
    )


def swap_bit(v, bit):
    count = lax.axis_size("fsdp")
    return lax.ppermute(v, "fsdp", [(i, i ^ (1 << bit)) for i in range(count)])


def halve(v, bits, left=None):
    count = lax.axis_size("fsdp").bit_length() - 1
    place = lax.axis_index("fsdp")
    left = list(range(count)) if left is None else list(left)
    for bit in bits:
        axis = len(left) - 1 - left.index(bit)
        left.remove(bit)
        mine = (place >> bit) & 1
        kept = lax.dynamic_index_in_dim(v, mine, axis, False)
        sent = lax.dynamic_index_in_dim(v, 1 - mine, axis, False)
        v = kept + swap_bit(sent, bit)
    return v


def cut_bit(v, bit, left):
    axis = len(left) - 1 - list(left).index(bit)
    mine = (lax.axis_index("fsdp") >> bit) & 1
    kept = lax.dynamic_index_in_dim(v, mine, axis, False)
    return kept, lax.dynamic_index_in_dim(v, 1 - mine, axis, False)


def by_bits(v):
    bits = v.shape[0].bit_length() - 1
    return v.reshape((2,) * bits + v.shape[1:])


def tied(*values):
    return lax.optimization_barrier(values)


class Ring:
    def __init__(self, v):
        count = lax.axis_size("fsdp")
        self.chips = count // 2
        place = lax.axis_index("fsdp")
        self.chip, self.core = place // 2, place % 2
        self.walk = list(range(0, self.chips, 2)) + list(range(1, self.chips, 2))[::-1]
        self.here = jnp.where(self.chip % 2 == 0, self.chip // 2, self.chips - 1 - self.chip // 2)
        self.up = self.down = v
        self.steps = 0
        self.found = []
        self.put(0, v)

    def chip_at(self, step):
        spot = (self.here + step) % self.chips
        return jnp.where(spot < (self.chips + 1) // 2, 2 * spot, 2 * (self.chips - 1 - spot) + 1)

    def turn(self, block, way):
        pairs = [
            (self.walk[i] * 2 + c, self.walk[(i + way) % self.chips] * 2 + c)
            for i in range(self.chips)
            for c in range(2)
        ]
        return lax.ppermute(block, "fsdp", pairs)

    def put(self, step, block):
        source = self.chip_at(step) * 2
        self.found.append((source + self.core, block))
        self.found.append((source + 1 - self.core, swap_bit(block, 0)))

    def step(self):
        self.steps += 1
        if 2 * self.steps < self.chips:
            self.up = self.turn(self.up, 1)
            self.down = self.turn(self.down, -1)
            self.put(-self.steps, self.up)
            self.put(self.steps, self.down)
        elif 2 * self.steps == self.chips:
            self.put(self.steps, self.turn(self.up, 1))

    def run(self, steps):
        for _ in range(steps):
            self.step()
        return self.found


def seq_swap(v):
    return lax.ppermute(v, "seq", [(0, 1), (1, 0)])


def seq_gather(v):
    if lax.axis_size("seq") != 2:
        return lax.all_gather(v, "seq", axis=0)
    other = seq_swap(v)
    low = lax.axis_index("seq") == 0
    return jnp.stack([jnp.where(low, v, other), jnp.where(low, other, v)])


def seq_parts(v):
    if lax.axis_size("seq") != 2:
        return None, lax.psum_scatter(v, "seq", scatter_dimension=0, tiled=True)
    place = lax.axis_index("seq")
    size = v.shape[0] // 2
    sent = lax.dynamic_slice_in_dim(v, (1 - place) * size, size, 0)
    return lax.dynamic_slice_in_dim(v, place * size, size, 0), seq_swap(sent)


def widen(v, width):
    if v.shape[-1] == width:
        return v
    return jnp.pad(v, [(0, 0)] * (v.ndim - 1) + [(0, width - v.shape[-1])])


def body(
    block_in,
    grad_out,
    doc_starts,
    in_weight,
    out_weight,
    conv_weight,
    conv_bias,
    norm_gain,
    gate_gain,
    decay_log,
    skip_gain,
    step_bias,
):
    seqs = lax.axis_size("seq")
    owners = lax.axis_size("fsdp")
    place = lax.axis_index("seq")
    rows_here, model = block_in.shape[1:]
    length = rows_here * seqs
    heads = decay_log.shape[0]
    heads_here = heads // seqs
    inner = out_weight.shape[0] * owners
    channels = conv_weight.shape[1] * owners
    states = channels - inner
    cg = heads_here * HEAD
    cp = -(-cg // LANES) * LANES
    cc = cp + states
    starts = doc_starts[0]

    shard, per = in_weight.shape[0], conv_bias.shape[0]
    place_row = place.reshape(1).astype(jnp.int32)
    out_piece = lax.dynamic_index_in_dim(out_weight.reshape(seqs, cg // owners, model), place, 0, False)
    out_piece = lax.ppermute(
        out_piece,
        ("seq", "fsdp"),
        [(s * owners + h, seqs * h + s) for s in range(seqs) for h in range(owners)],
    )
    own = pack_rows(
        seqs,
        place_row,
        in_weight,
        out_piece.reshape(shard, cg),
        conv_weight,
        conv_bias[None],
        norm_gain[None],
        gate_gain[None],
        states,
    )
    ring = Ring(own)
    if seqs == 2:
        tokens, others = block_in[0], seq_swap(block_in[0])
    else:
        tokens = others = lax.all_gather(block_in[0], "seq", axis=0, tiled=True)
    ring.run(min(2, owners // 4))
    grads = grad_out[0]
    ring.up, grads = tied(ring.up, grads)
    if seqs == 2:
        other_grads = seq_swap(grads)
    else:
        grads = other_grads = lax.all_gather(grads, "seq", axis=0, tiled=True)
    found = ring.run(owners // 4 - ring.steps)
    if cg == cp and cg // owners == shard and shard % 16 == 0:
        places = jnp.stack([spot for spot, _ in found])
        normed, gate, conv_in, act, slope, step, weights, out_rows, taps, norm_row, gain_row = enter_rows(
            seqs, per, starts, place_row, places, tokens, others, [v for _, v in found], None, None, None,
            length, cp, cc, inner,
        )
    else:
        gathered = jnp.zeros((owners,) + own.shape, BF16)
        for spot, v in found:
            gathered = lax.dynamic_update_index_in_dim(gathered, v, spot, 0)
        weights = gathered[:, :, : cp + cc + LANES].reshape(model, -1)
        out_rows = gathered[:, :, cp + cc + LANES : cp + cc + LANES + cg].reshape(cg, model)
        out_rows = jnp.pad(out_rows, ((0, cp - cg), (0, 0)))
        sides = gathered[:, :8, cp + cc + LANES - per : cp + cc + LANES].astype(F32)
        taps = sides.transpose(1, 0, 2).reshape(8, channels)
        taps = jnp.concatenate(
            [widen(lax.dynamic_slice_in_dim(taps, place * cg, cg, 1), cp), taps[:, inner:]], axis=1
        )
        norm_row = sides[:, TAPS + 1, :shard].reshape(1, model)
        gain_row = sides[:, TAPS + 2, : gate_gain.shape[0]].reshape(1, inner)
        gain_row = widen(lax.dynamic_slice_in_dim(gain_row, place * cg, cg, 1), cp)
        normed, gate, conv_in, act, slope, step = enter_rows(
            seqs, per, starts, place_row, None, tokens, others, None, norm_row, weights, taps, length, cp, cc, inner
        )

    def my_heads(v):
        return lax.dynamic_slice_in_dim(v, place * heads_here, heads_here)

    skip_row = widen(jnp.repeat(my_heads(skip_gain), HEAD)[None], cp)
    many = -(-(cp // HEAD) // 8) * 8

    def by_heads(v):
        return jnp.broadcast_to(widen(my_heads(v)[None], many).reshape(many, 1), (many, BLOCK))

    decay_row, step_row = by_heads(decay_log), by_heads(step_bias)

    y, mixed, dy, grads, partial_out, stats, states_kept = mix_rows(
        seqs, starts, place_row, act, gate, step, grads, other_grads, out_rows, gain_row, skip_row, step_row, decay_row
    )
    if seqs == 2:
        more = seq_swap(stats)
    else:
        stats, more = lax.psum(stats, "seq"), jnp.zeros_like(stats)
    out_kept, out_got = seq_parts(partial_out)

    bits = owners.bit_length() - 1
    dgate, dmix, gate_normed = ungate_rows(inner, stats, more, gate, mixed, dy, gain_row)
    early = by_bits(
        jnp.concatenate(
            [
                dot_tn(normed, dgate).astype(BF16).reshape(owners, shard, cp),
                dot_tn(gate_normed, grads).astype(BF16)[:cg].reshape(owners, shard, cg),
            ],
            axis=2,
        )
    )
    early_kept, early_got = cut_bit(early, 1, range(bits))
    early_got = swap_bit(early_got, 1)
    dproj, small_grads = unmix_rows(
        seqs, per, owners, starts, place_row, act, step, dmix, y, states_kept, slope, conv_in, taps,
        skip_row, step_row, decay_row,
    )
    dproj, early_got, out_got = tied(dproj, early_got, out_got)
    late = dot_tn(normed, dproj).astype(BF16).reshape(owners, shard, cc + LANES)
    late = late + jnp.pad(small_grads.astype(BF16), ((0, 0), (0, shard - 8), (cc, 0)))
    late = halve(by_bits(late), [0])
    late, late_got = cut_bit(late, 1, range(1, bits))
    late_got, early_kept, early_got = tied(late_got, early_kept, early_got)
    late_got = swap_bit(late_got, 1)
    early = halve(early_kept + early_got, [0], [0, *range(2, bits)])
    early, early_got = cut_bit(early, 2, range(2, bits))
    early_got, dgate = tied(early_got, dgate)
    early = early + swap_bit(early_got, 2)
    if seqs == 2:
        sent = back_rows(1 - place_row, 2, dgate, dproj, weights)
        sent, dgate = tied(sent, dgate)
        kept = back_rows(place_row, 2, dgate, dproj, weights)
        got = seq_swap(sent)
    else:
        d_normed = back_rows(jnp.zeros_like(place_row), 1, dgate, dproj, weights)
        kept, got = d_normed, lax.psum_scatter(d_normed, "seq", scatter_dimension=0, tiled=True)
    late_got, kept = tied(late_got, kept)
    late, late_got = cut_bit(late + late_got, 2, range(2, bits))
    late_got, early, kept, out_got = tied(late_got, early, kept, out_got)
    late = late + swap_bit(late_got, 2)
    early = halve(early, range(3, bits), range(3, bits))
    late, late_got = cut_bit(late, 3, range(3, bits))
    late_got, early = tied(late_got, early)
    late = halve(late + swap_bit(late_got, 3), range(4, bits), range(4, bits))
    piece = early[:, cp:].reshape(cg // owners, model)
    found = []
    for turn in range(seqs):
        pairs = []
        for q in range(seqs * owners):
            pairs.append((q, ((q + turn) % seqs) * owners + q // seqs))
        found.append(lax.ppermute(piece, ("seq", "fsdp"), pairs))
    late, got, found[0] = tied(late, got, found[0])
    mine = jnp.concatenate([early[:, :cp], late], axis=1)
    if seqs == 2:
        shares = [mine, seq_swap(mine)]
    else:
        shares = lax.all_gather(mine, "seq", axis=0)
        shares = [shares[i] for i in range(seqs)]
    in_grad, norm_grad, taps_grad, bias_grad, *head_grads = finish_rows(
        seqs, per, place_row, shares, in_weight, norm_gain, heads, cg, cp, cc
    )

    def total(kept, got):
        return kept.astype(F32) + got.astype(F32) if seqs == 2 else got.astype(F32)

    squares = lax.dynamic_slice_in_dim(stats[0] + more[0], place * rows_here, rows_here)
    out_scale = lax.rsqrt(squares / inner + EPS)
    block_out = (block_in[0].astype(F32) + out_scale[:, None] * total(out_kept, out_got)).astype(BF16)[None]
    d_normed_mine = total(kept, got)

    found = jnp.stack(found)
    out_grad = jnp.concatenate(
        [lax.dynamic_index_in_dim(found, (place - i) % seqs, 0, False) for i in range(seqs)], axis=0
    ).astype(F32)
    gain_grad = jnp.sum(out_grad * out_weight.astype(F32), axis=1) / gate_gain.astype(F32)

    x = block_in[0].astype(F32)
    scale = lax.rsqrt(jnp.mean(x * x, axis=-1, keepdims=True) + EPS)
    gained = d_normed_mine * norm_row
    along = scale * scale * jnp.mean(gained * x, axis=-1, keepdims=True)
    grad_in = (grad_out[0].astype(F32) + scale * (gained - x * along)).astype(BF16)[None]

    return (
        block_out,
        grad_in,
        in_grad,
        out_grad,
        taps_grad,
        bias_grad[0],
        norm_grad[0],
        gain_grad,
        head_grads[0][0],
        head_grads[2][0],
        head_grads[1][0],
    )


def solution(mesh):
    placed = (
        P("fsdp", "seq", None),
        P("fsdp", "seq", None),
        P("fsdp", None),
        P("fsdp", None),
        P("fsdp", None),
        P(None, "fsdp"),
        P("fsdp"),
        P("fsdp"),
        P("fsdp"),
        P(),
        P(),
        P(),
    )
    return jax.shard_map(
        body,
        mesh=mesh,
        in_specs=placed,
        out_specs=(
            P("fsdp", "seq", None),
            P("fsdp", "seq", None),
            P("fsdp", None),
            P("fsdp", None),
            P(None, "fsdp"),
            P("fsdp"),
            P("fsdp"),
            P("fsdp"),
            P(),
            P(),
            P(),
        ),
        check_vma=False,
    )
```
